32 devices in a mesh: shots: 2 (over x), slab: 16 (over z, y, core).
Axes of the slice: x: 2, y: 2, z: 4, core: 2. Of those that a mesh axis runs over, the one named last changes fastest.
Arguments:
- fields: float32 [32, 2, 2, 128, 256], P(('shots', 'slab')), parts along dimension 0, may hold values from -6 to 6
- freq_index: int32 [32], P(('shots', 'slab')), parts along dimension 0, may hold values from 0 to 511
- slowness_index: int32 [16, 128, 256], P('slab'), may hold values from 0 to 255
- slowness_table: float32 [256], replicated, may hold values from 1.2 to 2.4
Outputs:
- image: float32 [32, 128, 256], P(('shots', 'slab')), parts along dimension 0
- fields_out: float32 [32, 2, 2, 128, 256], P(('shots', 'slab')), parts along dimension 0
The draws below stay inside these ranges and needn't reach their ends.
There are 2 independent parts, one for each index of `shots`. The reference program is written for one: setup_inputs(seed, part) draws one part's arguments, and reference() takes and returns one part's arrays. A program takes and returns all parts, laid end to end along the dimension named above; an argument that names none is the same for every part. Nothing has to cross between parts.
All inputs are finite; a program needn't handle non-finite values.
Results may differ from the reference program's by a relative error of at most 0.0003.
Values sent between devices are 32-bit elements; how exact they have to be, the bound alone decides.
No kernel may reach another device: no remote copies, remote signals or barrier semaphores. Data moves between devices by JAX's collectives and lax.ppermute only.
A program may use at most 64 MiB of HBM per device.

```python
import jax
import jax.numpy as jnp
from jax import lax

NX = 128
NY = 256
STEPS = 1
TICKS = 3
LEVELS = 256
NFREQ = 512
ITEMS = 16
DEPTH = 16


def touch_ends(values, own_key, low, high):
    spot = [jax.random.randint(jax.random.fold_in(own_key, axis), (), 0, length) for axis, length in enumerate(values.shape)]
    widest = values.shape.index(max(values.shape))
    neighbour = spot[:widest] + [(spot[widest] + 1) % values.shape[widest]] + spot[widest + 1:]
    return values.at[tuple(spot)].set(low).at[tuple(neighbour)].set(high)


def levels(own_key, extent, cuts, least, top_value):
    def one(position, shards_of):
        steps = jax.random.uniform(jax.random.fold_in(jax.random.fold_in(own_key, 6), position), (shards_of,), jnp.float32, least / len(cuts), top_value / len(cuts))
        return jnp.repeat(jnp.exp(steps), extent[position] // shards_of).reshape((-1,) + (1,) * (len(extent) - position - 1))

    factor_of = one(*cuts[0])
    for cut in cuts[1:]:
        factor_of = factor_of * one(*cut)
    return factor_of


def noise(key, shape, deviation, most, split=(), kind=jnp.bfloat16):
    level = levels(key, shape, split, -0.22, 0.18) if split else 1.0
    values = jax.random.normal(key, shape, jnp.float32) * deviation * level
    return jnp.minimum(jnp.maximum(values, -most), most).astype(kind)


def setup_inputs(seed: int = 0, part: int = 0) -> dict:
    key_list = jax.random.split(jax.random.key(seed), 5)
    own_keys = jax.random.split(jax.random.fold_in(key_list[4], part), 5)
    fields = noise(own_keys[0], (ITEMS, 2, 2, NX, NY), 1.0, 6.0, ((0, 16),), jnp.float32)
    freq_index = touch_ends(jax.random.randint(own_keys[1], (ITEMS,), 0, NFREQ), jax.random.fold_in(own_keys[1], 1), 0, NFREQ - 1).astype(jnp.int32)
    slowness_index = touch_ends(jax.random.randint(key_list[2], (DEPTH, NX, NY), 0, LEVELS), jax.random.fold_in(key_list[2], 1), 0, LEVELS - 1).astype(jnp.int32)
    slowness_table = jnp.clip(jax.random.uniform(key_list[3], (LEVELS,), jnp.float32, 1.2, 2.4), 1.2, 2.4)
    return {"fields": fields, "freq_index": freq_index, "slowness_index": slowness_index, "slowness_table": slowness_table}


def advance(real_part, imag_part, omega, plane, mean_slow, signs, wave_sq):
    spectrum = jnp.fft.fft2(lax.complex(real_part, imag_part))
    spec_real = jnp.real(spectrum)
    spec_imag = jnp.imag(spectrum)
    k_square = (omega * mean_slow) ** 2
    vertical = jnp.sqrt(jnp.maximum(k_square - wave_sq, 0.0))
    decay = jnp.sqrt(jnp.maximum(wave_sq - k_square, 0.0))
    damping = jnp.exp(-decay)
    cosine = damping * jnp.cos(vertical)
    sine = signs * damping * jnp.sin(vertical)
    shifted_real = spec_real * cosine - spec_imag * sine
    shifted_imag = spec_real * sine + spec_imag * cosine
    back = jnp.fft.ifft2(lax.complex(shifted_real, shifted_imag))
    back_real = jnp.real(back)
    back_imag = jnp.imag(back)
    screen = omega * (plane - mean_slow)
    screen_cos = jnp.cos(screen)
    screen_sin = signs * jnp.sin(screen)
    return (back_real * screen_cos - back_imag * screen_sin, back_real * screen_sin + back_imag * screen_cos)

def reference(fields, freq_index, slowness_index, slowness_table):
    slow = jnp.take(slowness_table, slowness_index, axis=0)
    mean_slow = lax.optimization_barrier(jnp.mean(slow, axis=(1, 2)))
    planes = slow.reshape(ITEMS, STEPS, NX, NY)
    means = mean_slow.reshape(ITEMS, STEPS)
    omega = 1.0 + freq_index.astype(jnp.float32) / NFREQ
    wave_x = jnp.fft.fftfreq(NX).astype(jnp.float32) * (2.0 * jnp.pi)
    wave_y = jnp.fft.fftfreq(NY).astype(jnp.float32) * (2.0 * jnp.pi)
    wave_sq = wave_x[:, None] ** 2 + wave_y[None, :] ** 2
    signs = jnp.array([1.0, -1.0], dtype=jnp.float32).reshape(2, 1, 1)

    def slab_pass(inputs):
        state, frequency, slab_planes, slab_means = inputs
        real_part = state[:, 0]
        imag_part = state[:, 1]
        images = []
        for depth_no in range(STEPS):
            real_part, imag_part = advance(real_part, imag_part, frequency, slab_planes[depth_no], slab_means[depth_no], signs, wave_sq)
            images.append(real_part[0] * real_part[1] + imag_part[0] * imag_part[1])
        return (jnp.stack([real_part, imag_part], axis=1), jnp.stack(images))
    state = fields
    image_raw = jnp.zeros((DEPTH, NX, NY), dtype=jnp.float32)
    for tick_no in range(TICKS):
        if tick_no > 0:
            state = jnp.concatenate([jnp.zeros_like(state[:1]), state[:-1]], axis=0)
            omega = jnp.concatenate([jnp.zeros_like(omega[:1]), omega[:-1]], axis=0)
        state, added = lax.map(slab_pass, (state, omega, planes, means))
        image_raw = image_raw + added.reshape(DEPTH, NX, NY)
    padded = jnp.pad(image_raw, ((1, 1), (0, 0), (0, 0)))
    image = image_raw - 0.25 * (padded[:-2] + padded[2:])
    return (image, state)
```

```python
import functools
import math

import jax
import jax.numpy as jnp
import ml_dtypes
import numpy as np
from jax import lax
from jax.experimental import pallas as pl
from jax.experimental.pallas import tpu as pltpu
from jax.sharding import PartitionSpec as P

TICKS = 3
NFREQ = 512
EXTRA = 8
LANES = 128
TABLES = 5
TWO_PI = 2.0 * math.pi


def split_table(angle):
    parts = np.concatenate([np.cos(angle), np.sin(angle)], axis=0)
    high = parts.astype(np.float32).astype(ml_dtypes.bfloat16)
    low = (parts - high.astype(np.float64)).astype(np.float32).astype(ml_dtypes.bfloat16)
    return np.concatenate([high, low], axis=0)


def x_order(rows):
    front = np.arange(rows // 2)
    return np.concatenate([front, [rows // 2], rows - front[1:]])


def dft_tables(rows, cols):
    x_no, y_no = np.arange(rows), np.arange(cols // 2)
    to_x = np.outer(x_order(rows), x_no) % rows * (TWO_PI / rows)
    even = np.outer(y_no, 2 * y_no) % cols * (TWO_PI / cols)
    to_odd = np.outer(y_no, 2 * y_no + 1) % cols * (TWO_PI / cols)
    return [split_table(angle) for angle in (to_x, to_x.T, even, to_odd, to_odd.T)]


def passes(value, axis):
    high = value.astype(jnp.bfloat16)
    low = (value - high.astype(jnp.float32)).astype(jnp.bfloat16)
    return jnp.concatenate([high, low, high], axis=axis)


def table_parts(table_ref, turn):
    size = table_ref.shape[1]
    parts = []
    for start in (0, 2 * size):
        cos = table_ref[start : start + size]
        sin = table_ref[start + size : start + 2 * size]
        if turn:
            parts.append(stack(side(cos, sin), side(-sin, cos)))
        else:
            parts.append(stack(side(cos, -sin), side(sin, cos)))
    return parts


def dot_right(value, table_ref):
    high, low = table_parts(table_ref, False)
    return jnp.dot(
        passes(value, 1), stack(high, high, low), preferred_element_type=jnp.float32
    )


def dot_left(table_ref, value):
    high, low = table_parts(table_ref, True)
    return jnp.dot(side(high, high, low), passes(value, 0), preferred_element_type=jnp.float32)


def cos_sin(angle):
    turns = jnp.floor(angle * (1.0 / math.pi) + 0.5)
    pairs = turns * 0.5
    flip = 1.0 - 4.0 * (pairs - jnp.floor(pairs))
    rest = angle - turns * math.pi
    sq = rest * rest
    sin = -1.98089830e-4 + sq * 2.60501962e-6
    sin = 8.33304978e-3 + sq * sin
    sin = -1.66666579e-1 + sq * sin
    sin = 9.99999996e-1 + sq * sin
    cos = -1.38535979e-3 + sq * 2.31515763e-5
    cos = 4.16635698e-2 + sq * cos
    cos = -4.99999047e-1 + sq * cos
    cos = 9.99999953e-1 + sq * cos
    return cos * flip, sin * (rest * flip)


def wave_square(rows, cols):
    half = cols // 2
    shape = (rows // 2 + EXTRA, cols)
    row = lax.broadcasted_iota(jnp.int32, shape, 0)
    row = jnp.where(row > rows // 2, rows // 2 - row, row)
    col = lax.broadcasted_iota(jnp.int32, shape, 1)
    col = jnp.where(col < half, 2 * col, 2 * (col - half) + 1)
    col = jnp.where(col < half, col, col - cols)
    wave_x = row.astype(jnp.float32) * (TWO_PI / rows)
    wave_y = col.astype(jnp.float32) * (TWO_PI / cols)
    return wave_x * wave_x + wave_y * wave_y


def depth_factor(omega_mean, wave_sq, rows, cols):
    gap = omega_mean * omega_mean - wave_sq
    root = jnp.sqrt(jnp.abs(gap))
    cos, sin = cos_sin(root)
    scale = 1.0 / (rows * cols)
    wave = gap > 0.0
    cos = jnp.where(wave, cos, jnp.exp(-root)) * scale
    sin = jnp.where(wave, sin, 0.0) * scale
    return [stack(part, part[EXTRA : rows // 2]) for part in (cos, sin)]


def side(*parts):
    return jnp.concatenate(parts, axis=1)


def stack(*parts):
    return jnp.concatenate(parts, axis=0)


def depth_step(fields, factor, screen, tables):
    left, left_back, even, odd, odd_back = tables
    spectra = []
    for real, imag in fields:
        half = real.shape[1] // 2
        first = side(real[:, :half], imag[:, :half])
        second = side(real[:, half:], imag[:, half:])
        spectra.append((dot_right(first + second, even), dot_right(first - second, odd)))
    spectra = [
        stack(side(low[:, :half], high[:, :half]), side(low[:, half:], high[:, half:]))
        for low, high in spectra
    ]
    spectra = [dot_left(left, spectrum) for spectrum in spectra]
    cos, sin = factor()
    rows = cos.shape[0]
    moved = []
    for spectrum in spectra:
        real, imag = spectrum[:rows], spectrum[rows:]
        moved.append(stack(real * sin + imag * cos, real * cos - imag * sin))
    backs = [dot_left(left_back, spectrum) for spectrum in moved]
    parts = []
    for back in backs:
        sum_part = dot_right(side(back[:rows, :half], back[rows:, :half]), even)
        gap_part = dot_right(side(back[:rows, half:], back[rows:, half:]), odd_back)
        parts.append((sum_part, gap_part))
    cos, sin = screen()
    results = []
    for sum_part, gap_part in parts:
        first, second = sum_part + gap_part, sum_part - gap_part
        real = side(first[:, half:], second[:, half:])
        imag = side(first[:, :half], second[:, :half])
        results.append((real * cos - imag * sin, real * sin + imag * cos))
    return results


def both_fields(state_ref, rows, factor, screen, tables):
    def fields():
        if len(state_ref.shape) == 2:
            parts = [state_ref[i * rows : (i + 1) * rows] for i in range(4)]
        else:
            parts = [state_ref[0, i, j] for i in range(2) for j in range(2)]
        s_real, s_imag, r_real, r_imag = parts
        return (s_real, s_imag), (r_imag, r_real)

    (s_real, s_imag), (r_imag, r_real) = depth_step(fields(), factor, screen, tables)
    return (s_real, s_imag, r_real, r_imag), s_real * r_real + s_imag * r_imag


def look_up(index, *tables):
    found = []
    for table in tables:
        pieces = []
        for start in range(0, index.shape[1], LANES):
            piece = index[:, start : start + LANES]
            value = jnp.zeros(piece.shape, jnp.float32)
            for low in range(0, table.shape[1], LANES):
                entries = jnp.broadcast_to(table[:, low : low + LANES], piece.shape)
                inside = jnp.clip(piece - low, 0, LANES - 1)
                picked = jnp.take_along_axis(entries, inside, axis=1)
                value = jnp.where(piece >= low, picked, value)
            pieces.append(value)
        found.append(side(*pieces))
    return found


def screen_of(index, omega, entries, mean):
    return look_up(index, *cos_sin(omega * (entries - mean)))


def store_planes(ref, planes):
    rows = planes[0].shape[0]
    for i, plane in enumerate(planes):
        ref[i * rows : (i + 1) * rows] = plane


def is_odd():
    return lax.rem(lax.axis_index("slab"), 2) == 1


def is_even():
    return jnp.logical_not(is_odd())


def load_and_step(operands, outputs, scratch):
    freq_hbm, fields_hbm, index_hbm, entries_hbm, *tables_hbm = operands
    state_ref, plane_ref, image_ref, wave_ref, levels_ref, *tables = outputs
    freq_ref, own_ref, index_ref, entries_ref, sems = scratch
    rows, cols = image_ref.shape
    pairs = [(fields_hbm, own_ref), (index_hbm, index_ref), (entries_hbm, entries_ref)]
    pairs += [(freq_hbm, freq_ref), *zip(tables_hbm, tables)]
    copies = [pltpu.make_async_copy(*pair, sems.at[i]) for i, pair in enumerate(pairs)]
    for copy in copies:
        copy.start()
    wave_sq = wave_square(rows, cols)
    wave_ref[...] = wave_sq
    for copy in copies:
        copy.wait()
    index, entries = index_ref[0], entries_ref[...]
    omega = 1.0 + freq_ref[0].astype(jnp.float32) * (1.0 / NFREQ)
    means = []

    def factor():
        (slow,) = look_up(index, entries)
        means.append(jnp.sum(slow, axis=(0, 1), keepdims=True) * (1.0 / (rows * cols)))
        return depth_factor(omega * means[0], wave_sq, rows, cols)

    planes, image = both_fields(
        own_ref, rows, factor, lambda: screen_of(index, omega, entries, means[0]), tables
    )
    store_planes(state_ref, planes)
    state_ref[4 * rows :] = jnp.full((state_ref.shape[0] - 4 * rows, cols), omega, jnp.float32)
    image_ref[...] = image
    plane_ref[:rows] = index.astype(jnp.float32)
    plane_ref[rows:] = jnp.broadcast_to(means[0], (EXTRA, cols))
    levels_ref[...] = jnp.broadcast_to(entries, levels_ref.shape)


def odd_first_kernel(*refs):
    operands, refs = refs[: 4 + TABLES], refs[4 + TABLES :]
    outputs, scratch = refs[: 5 + TABLES], refs[5 + TABLES :]
    pl.when(is_odd())(functools.partial(load_and_step, operands, outputs, scratch))


def even_first_kernel(*refs):
    operands, refs = refs[: 4 + TABLES], refs[4 + TABLES :]
    kept, refs = refs[: 4 + TABLES], refs[4 + TABLES :]
    outputs, scratch = refs[: 5 + TABLES], refs[5 + TABLES :]
    pl.when(is_even())(functools.partial(load_and_step, operands, outputs, scratch))

    @pl.when(is_odd())
    def _():
        for kept_ref, out_ref in zip(kept, outputs[1:]):
            out_ref[...] = kept_ref[...]


def step_from(state_ref, plane_ref, constants):
    wave_ref, levels_ref, *tables = constants
    rows = plane_ref.shape[0] - EXTRA
    omega = state_ref[4 * rows : 4 * rows + 1, :1]
    mean = plane_ref[rows : rows + 1, :1]
    index = plane_ref[:rows].astype(jnp.int32)
    return both_fields(
        state_ref,
        rows,
        lambda: depth_factor(omega * mean, wave_ref[...], rows, index.shape[1]),
        lambda: screen_of(index, omega, levels_ref[:1], mean),
        tables,
    )


def odd_second_kernel(state_in_ref, plane_ref, image_in_ref, *refs):
    constants, (state_ref, image_ref) = refs[: 2 + TABLES], refs[2 + TABLES :]
    rows = image_ref.shape[0]

    @pl.when(is_odd())
    def _():
        planes, image = step_from(state_in_ref, plane_ref, constants)
        store_planes(state_ref, planes)
        for start in range(4 * rows, state_ref.shape[0], EXTRA):
            state_ref[start : start + EXTRA] = state_in_ref[4 * rows :]
        image_ref[...] = image_in_ref[...] + image

    @pl.when(is_even())
    def _():
        image_ref[...] = image_in_ref[...]


def odd_ahead_kernel(state_in_ref, plane_ref, *refs):
    constants, (image_ref,) = refs[: 2 + TABLES], refs[2 + TABLES :]
    has_next = is_odd() & (lax.axis_index("slab") < lax.axis_size("slab") - 1)

    @pl.when(has_next)
    def _():
        _, image = step_from(state_in_ref, plane_ref, constants)
        image_ref[...] = image

    @pl.when(jnp.logical_not(has_next))
    def _():
        image_ref[...] = jnp.zeros_like(image_ref)


def fill_wide(ref, raw):
    rows = raw.shape[0]
    ref[:rows] = raw
    ref[rows:] = jnp.zeros((ref.shape[0] - rows, ref.shape[1]), jnp.float32)


def even_arrival_kernel(state_in_ref, plane_ref, image_in_ref, *refs):
    constants, (state_ref, image_ref, up_ref) = refs[: 2 + TABLES], refs[2 + TABLES :]
    rows = image_ref.shape[0]

    @pl.when(is_even())
    def _():
        planes, image = step_from(state_in_ref, plane_ref, constants)
        store_planes(state_ref, planes)
        state_ref[4 * rows :] = state_in_ref[4 * rows : 4 * rows + EXTRA]
        image = image_in_ref[...] + image
        image_ref[...] = image
        fill_wide(up_ref, image)

    @pl.when(is_odd())
    def _():
        image_ref[...] = image_in_ref[...]


def odd_last_kernel(state_in_ref, plane_ref, image_in_ref, ahead_ref, *refs):
    constants, (state_ref, raw_ref, base_ref) = refs[: 2 + TABLES], refs[2 + TABLES :]

    @pl.when(is_odd())
    def _():
        planes, image = step_from(state_in_ref, plane_ref, constants)
        store_planes(state_ref, planes)
        raw = image_in_ref[...] + image
        fill_wide(raw_ref, raw)
        base_ref[...] = raw - 0.25 * ahead_ref[...]


def even_last_kernel(
    state_in_ref, plane_ref, image_in_ref, odd_raw_ref, odd_base_ref, *refs
):
    constants, (state_ref, raw_ref, base_ref) = refs[: 2 + TABLES], refs[2 + TABLES :]

    @pl.when(is_even())
    def _():
        planes, image = step_from(state_in_ref, plane_ref, constants)
        store_planes(state_ref, planes)
        raw = image_in_ref[...] + image
        raw_ref[...] = raw
        base_ref[...] = raw

    @pl.when(is_odd())
    def _():
        raw_ref[...] = odd_raw_ref[: raw_ref.shape[0]]
        base_ref[...] = odd_base_ref[...]


def write_kernel(odd_ref, even_ref, fields_hbm, done_ref, sems):
    rows = even_ref.shape[0] // 4

    def write(ref):
        copies = [
            pltpu.make_async_copy(
                ref.at[pl.ds(i * rows, rows)], fields_hbm.at[0, i // 2, i % 2], sems.at[i]
            )
            for i in range(4)
        ]
        for copy in copies:
            copy.start()
        for copy in copies:
            copy.wait()

    pl.when(is_odd())(functools.partial(write, odd_ref))
    pl.when(is_even())(functools.partial(write, even_ref))
    done_ref[...] = jnp.zeros_like(done_ref)


def stencil_kernel(base_ref, below_ref, above_ref, swap_ref, done_ref, image_ref):
    del done_ref
    rows = base_ref.shape[0]
    off = below_ref[:rows] + above_ref[:rows]
    image_ref[0] = base_ref[...] - 0.25 * (swap_ref[...] + off)


def body(fields, freq_index, slowness_index, slowness_table):
    rows, cols = slowness_index.shape[1:]
    slabs = lax.axis_size("slab")
    on_pairs = [(i, i + 1) for i in range(0, slabs - 1, 2)]
    off_pairs = [(i, i + 1) for i in range(1, slabs - 1, 2)]
    on_back = [(j, i) for i, j in on_pairs]
    off_back = [(j, i) for i, j in off_pairs]

    f32 = jnp.float32
    vmem = pl.BlockSpec(memory_space=pltpu.VMEM)
    hbm = pl.BlockSpec(memory_space=pltpu.HBM)
    products = 24 * (2 * rows) * cols * cols
    cost = pl.CostEstimate(flops=2 * products, bytes_accessed=16 * rows * cols * 4, transcendentals=0)

    long = pl.CostEstimate(
        flops=10 * 2 * products, bytes_accessed=10 * 16 * rows * cols * 4, transcendentals=0
    )

    def shape_of(height):
        return jax.ShapeDtypeStruct((height, cols), f32)

    def call(kernel, name, operands, out_shapes, cost=cost, **rest):
        rest.setdefault("in_specs", [vmem] * len(operands))
        rest.setdefault("out_specs", (vmem,) * len(out_shapes))
        return pl.pallas_call(
            kernel,
            out_shape=tuple(out_shapes),
            compiler_params=pltpu.CompilerParams(vmem_limit_bytes=32 * 1024 * 1024),
            cost_estimate=cost,
            name=name,
            **rest,
        )(*operands)

    long_state_shape = shape_of(4 * rows + 2 * EXTRA)
    state_shape, plane_shape, image_shape = shape_of(4 * rows + EXTRA), shape_of(rows + EXTRA), shape_of(rows)
    tables = [jnp.asarray(table) for table in dft_tables(rows, cols)]
    table_shapes = [jax.ShapeDtypeStruct(t.shape, t.dtype) for t in tables]
    levels_shape = jax.ShapeDtypeStruct((EXTRA,) + slowness_table.shape, f32)
    kept_shapes = [plane_shape, image_shape, shape_of(rows // 2 + EXTRA), levels_shape] + table_shapes
    loaded = (fields, slowness_index, slowness_table[None], *tables)
    operands = (freq_index,) + tuple(
        pltpu.with_memory_space_constraint(x, pltpu.HBM) for x in loaded
    )
    scratch = [
        pltpu.SMEM(freq_index.shape, freq_index.dtype),
        pltpu.VMEM(fields.shape, f32),
        pltpu.VMEM(slowness_index.shape, slowness_index.dtype),
        pltpu.VMEM((1,) + slowness_table.shape, f32),
        pltpu.SemaphoreType.DMA((4 + TABLES,)),
    ]
    odd_state, *kept = call(
        odd_first_kernel, "odd_first_step", operands, [long_state_shape] + kept_shapes,
        in_specs=[hbm] * len(operands), scratch_shapes=scratch,
    )
    from_off = lax.ppermute(odd_state, "slab", off_pairs)
    even_state, plane, image, *constants = call(
        even_first_kernel, "even_first_step", (*operands, *kept), [state_shape] + kept_shapes,
        in_specs=[hbm] * len(operands) + [vmem] * len(kept), scratch_shapes=scratch,
    )
    from_on = lax.ppermute(even_state, "slab", on_pairs)
    next_plane = lax.ppermute(plane, "slab", off_back)
    odd_state, image = call(
        odd_second_kernel, "odd_second_step", (from_on, plane, image, *constants),
        [shape_of(4 * rows + 3 * EXTRA), image_shape], cost=None,
    )
    last_off = lax.ppermute(odd_state, "slab", off_pairs)
    even_state, image, up_image = call(
        even_arrival_kernel, "even_arrival_step", (from_off, plane, image, *constants),
        [state_shape, image_shape, shape_of(rows + 2 * EXTRA)],
    )
    last_on = lax.ppermute(even_state, "slab", on_pairs)
    below = lax.ppermute(up_image, "slab", off_back)
    (ahead,) = call(
        odd_ahead_kernel, "odd_step_ahead", (odd_state, next_plane, *constants), [image_shape],
        cost=long,
    )
    odd_fields, odd_raw, odd_base = call(
        odd_last_kernel, "odd_last_step", (last_on, plane, image, ahead, *constants),
        [shape_of(4 * rows), shape_of(rows + EXTRA), image_shape], cost=None,
    )
    above = lax.ppermute(odd_raw, "slab", off_pairs)
    even_fields, raw, base = call(
        even_last_kernel, "even_last_step",
        (last_off, plane, image, odd_raw, odd_base, *constants),
        [shape_of(4 * rows), image_shape, image_shape], cost=None,
    )
    swapped = lax.ppermute(raw, "slab", on_pairs + on_back)
    fields_out, done = call(
        write_kernel, "write_fields", (odd_fields, even_fields),
        [jax.ShapeDtypeStruct(fields.shape, f32), jax.ShapeDtypeStruct((EXTRA, LANES), f32)],
        out_specs=(hbm, vmem), scratch_shapes=[pltpu.SemaphoreType.DMA((4,))], cost=None,
    )
    (image,) = call(
        stencil_kernel, "image_stencil", (base, below, above, swapped, done),
        [jax.ShapeDtypeStruct((1, rows, cols), f32)], cost=None,
    )
    return image, fields_out


def solution(mesh):
    return jax.shard_map(
        body,
        mesh=mesh,
        in_specs=(
            P(("shots", "slab"), None, None, None, None),
            P(("shots", "slab")),
            P("slab", None, None),
            P(),
        ),
        out_specs=(P(("shots", "slab"), None, None), P(("shots", "slab"), None, None, None, None)),
        check_vma=False,
    )
```

```python
import functools
import math

import jax
import jax.numpy as jnp
import ml_dtypes
import numpy as np
from jax import lax
from jax.experimental import pallas as pl
from jax.experimental.pallas import tpu as pltpu
from jax.sharding import PartitionSpec as P

TICKS = 3
NFREQ = 512
EXTRA = 8
LANES = 128
TABLES = 2
TWO_PI = 2.0 * math.pi


def split_table(angle):
    parts = np.concatenate([np.cos(angle), np.sin(angle)], axis=0)
    high = parts.astype(np.float32).astype(ml_dtypes.bfloat16)
    low = (parts - high.astype(np.float64)).astype(np.float32).astype(ml_dtypes.bfloat16)
    return np.concatenate([high, low], axis=0)


def x_order(rows):
    front = np.arange(rows // 2)
    return np.concatenate([front, [rows // 2], rows - front[1:]])


def dft_tables(rows, cols):
    x_no, y_no = np.arange(rows), np.arange(cols // 2)
    to_x = np.outer(x_order(rows), x_no) % rows * (TWO_PI / rows)
    even = np.outer(y_no, 2 * y_no) % cols * (TWO_PI / cols)
    to_odd = np.outer(y_no, 2 * y_no + 1) % cols * (TWO_PI / cols)
    groups = ((to_x, to_x.T), (even, to_odd, to_odd.T))
    return [np.concatenate([split_table(angle) for angle in group]) for group in groups]


def table_views(x_ref, y_ref):
    views = []
    for ref, count in ((x_ref, 2), (y_ref, 3)):
        size = 4 * ref.shape[1]
        views += [ref.at[pl.ds(i * size, size)] for i in range(count)]
    return views


def passes(value, axis):
    high = value.astype(jnp.bfloat16)
    low = (value - high.astype(jnp.float32)).astype(jnp.bfloat16)
    return jnp.concatenate([high, low, high], axis=axis)


def table_parts(table_ref, turn):
    size = table_ref.shape[1]
    parts = []
    for start in (0, 2 * size):
        cos = table_ref[start : start + size]
        sin = table_ref[start + size : start + 2 * size]
        if turn:
            parts.append(stack(side(cos, sin), side(-sin, cos)))
        else:
            parts.append(stack(side(cos, -sin), side(sin, cos)))
    return parts


def dot_right(value, table_ref):
    high, low = table_parts(table_ref, False)
    return jnp.dot(
        passes(value, 1), stack(high, high, low), preferred_element_type=jnp.float32
    )


def dot_left(table_ref, value):
    high, low = table_parts(table_ref, True)
    return jnp.dot(side(high, high, low), passes(value, 0), preferred_element_type=jnp.float32)


def cos_sin(angle):
    turns = jnp.floor(angle * (1.0 / math.pi) + 0.5)
    pairs = turns * 0.5
    flip = 1.0 - 4.0 * (pairs - jnp.floor(pairs))
    rest = angle - turns * math.pi
    sq = rest * rest
    sin = -1.98089830e-4 + sq * 2.60501962e-6
    sin = 8.33304978e-3 + sq * sin
    sin = -1.66666579e-1 + sq * sin
    sin = 9.99999996e-1 + sq * sin
    cos = -1.38535979e-3 + sq * 2.31515763e-5
    cos = 4.16635698e-2 + sq * cos
    cos = -4.99999047e-1 + sq * cos
    cos = 9.99999953e-1 + sq * cos
    return cos * flip, sin * (rest * flip)


def wave_square(rows, cols):
    half = cols // 2
    shape = (rows // 2 + EXTRA, cols)
    row = lax.broadcasted_iota(jnp.int32, shape, 0)
    row = jnp.where(row > rows // 2, rows // 2 - row, row)
    col = lax.broadcasted_iota(jnp.int32, shape, 1)
    col = jnp.where(col < half, 2 * col, 2 * (col - half) + 1)
    col = jnp.where(col < half, col, col - cols)
    wave_x = row.astype(jnp.float32) * (TWO_PI / rows)
    wave_y = col.astype(jnp.float32) * (TWO_PI / cols)
    return wave_x * wave_x + wave_y * wave_y


def depth_factor(omega_mean, wave_sq, rows, cols):
    gap = omega_mean * omega_mean - wave_sq
    root = jnp.sqrt(jnp.abs(gap))
    cos, sin = cos_sin(root)
    scale = 1.0 / (rows * cols)
    wave = gap > 0.0
    cos = jnp.where(wave, cos, jnp.exp(-root)) * scale
    sin = jnp.where(wave, sin, 0.0) * scale
    return [stack(part, part[EXTRA : rows // 2]) for part in (cos, sin)]


def side(*parts):
    return jnp.concatenate(parts, axis=1)


def stack(*parts):
    return jnp.concatenate(parts, axis=0)


def depth_step(fields, factor, screen, tables):
    left, left_back, even, odd, odd_back = table_views(*tables)
    spectra = []
    for real, imag in fields:
        half = real.shape[1] // 2
        first = side(real[:, :half], imag[:, :half])
        second = side(real[:, half:], imag[:, half:])
        spectra.append((dot_right(first + second, even), dot_right(first - second, odd)))
    spectra = [
        stack(side(low[:, :half], high[:, :half]), side(low[:, half:], high[:, half:]))
        for low, high in spectra
    ]
    spectra = [dot_left(left, spectrum) for spectrum in spectra]
    cos, sin = factor()
    rows = cos.shape[0]
    moved = []
    for spectrum in spectra:
        real, imag = spectrum[:rows], spectrum[rows:]
        moved.append(stack(real * sin + imag * cos, real * cos - imag * sin))
    backs = [dot_left(left_back, spectrum) for spectrum in moved]
    parts = []
    for back in backs:
        sum_part = dot_right(side(back[:rows, :half], back[rows:, :half]), even)
        gap_part = dot_right(side(back[:rows, half:], back[rows:, half:]), odd_back)
        parts.append((sum_part, gap_part))
    cos, sin = screen()
    results = []
    for sum_part, gap_part in parts:
        first, second = sum_part + gap_part, sum_part - gap_part
        real = side(first[:, half:], second[:, half:])
        imag = side(first[:, :half], second[:, :half])
        results.append((real * cos - imag * sin, real * sin + imag * cos))
    return results


def both_fields(state_ref, rows, factor, screen, tables):
    def fields():
        if len(state_ref.shape) == 2:
            parts = [state_ref[i * rows : (i + 1) * rows] for i in range(4)]
        else:
            parts = [state_ref[0, i, j] for i in range(2) for j in range(2)]
        s_real, s_imag, r_real, r_imag = parts
        return (s_real, s_imag), (r_imag, r_real)

    (s_real, s_imag), (r_imag, r_real) = depth_step(fields(), factor, screen, tables)
    return (s_real, s_imag, r_real, r_imag), s_real * r_real + s_imag * r_imag


def look_up(index, *tables):
    found = []
    for table in tables:
        pieces = []
        for start in range(0, index.shape[1], LANES):
            piece = index[:, start : start + LANES]
            value = jnp.zeros(piece.shape, jnp.float32)
            for low in range(0, table.shape[1], LANES):
                entries = jnp.broadcast_to(table[:, low : low + LANES], piece.shape)
                inside = jnp.clip(piece - low, 0, LANES - 1)
                picked = jnp.take_along_axis(entries, inside, axis=1)
                value = jnp.where(piece >= low, picked, value)
            pieces.append(value)
        found.append(side(*pieces))
    return found


def screen_of(index, omega, entries, mean):
    return look_up(index, *cos_sin(omega * (entries - mean)))


def store_planes(ref, planes):
    rows = planes[0].shape[0]
    for i, plane in enumerate(planes):
        ref[i * rows : (i + 1) * rows] = plane


def is_odd():
    return lax.rem(lax.axis_index("slab"), 2) == 1


def is_even():
    return jnp.logical_not(is_odd())


def load_and_step(operands, outputs, scratch):
    freq_hbm, fields_hbm, index_hbm, entries_hbm, *tables_hbm = operands
    state_ref, plane_ref, image_ref, wave_ref, levels_ref, *tables = outputs
    freq_ref, own_ref, index_ref, entries_ref, sems = scratch
    rows, cols = image_ref.shape
    pairs = [(fields_hbm, own_ref), (index_hbm, index_ref), (entries_hbm, entries_ref)]
    pairs += [(freq_hbm, freq_ref), *zip(tables_hbm, tables)]
    copies = [pltpu.make_async_copy(*pair, sems.at[i]) for i, pair in enumerate(pairs)]
    for copy in copies:
        copy.start()
    wave_sq = wave_square(rows, cols)
    wave_ref[...] = wave_sq
    for copy in copies:
        copy.wait()
    index, entries = index_ref[0], entries_ref[...]
    omega = 1.0 + freq_ref[0].astype(jnp.float32) * (1.0 / NFREQ)
    means = []

    def factor():
        (slow,) = look_up(index, entries)
        means.append(jnp.sum(slow, axis=(0, 1), keepdims=True) * (1.0 / (rows * cols)))
        return depth_factor(omega * means[0], wave_sq, rows, cols)

    planes, image = both_fields(
        own_ref, rows, factor, lambda: screen_of(index, omega, entries, means[0]), tables
    )
    store_planes(state_ref, planes)
    state_ref[4 * rows :] = jnp.full((state_ref.shape[0] - 4 * rows, cols), omega, jnp.float32)
    image_ref[...] = image
    plane_ref[:rows] = index.astype(jnp.float32)
    plane_ref[rows:] = jnp.broadcast_to(means[0], (EXTRA, cols))
    levels_ref[...] = jnp.broadcast_to(entries, levels_ref.shape)


def odd_first_kernel(*refs):
    operands, refs = refs[: 4 + TABLES], refs[4 + TABLES :]
    outputs, scratch = refs[: 5 + TABLES], refs[5 + TABLES :]
    pl.when(is_odd())(functools.partial(load_and_step, operands, outputs, scratch))


def even_first_kernel(*refs):
    operands, refs = refs[: 4 + TABLES], refs[4 + TABLES :]
    kept, refs = refs[: 4 + TABLES], refs[4 + TABLES :]
    outputs, scratch = refs[: 5 + TABLES], refs[5 + TABLES :]
    pl.when(is_even())(functools.partial(load_and_step, operands, outputs, scratch))

    @pl.when(is_odd())
    def _():
        for kept_ref, out_ref in zip(kept, outputs[1:]):
            out_ref[...] = kept_ref[...]


def step_from(state_ref, plane_ref, constants):
    wave_ref, levels_ref, *tables = constants
    rows = plane_ref.shape[0] - EXTRA
    omega = state_ref[4 * rows : 4 * rows + 1, :1]
    mean = plane_ref[rows : rows + 1, :1]
    index = plane_ref[:rows].astype(jnp.int32)
    return both_fields(
        state_ref,
        rows,
        lambda: depth_factor(omega * mean, wave_ref[...], rows, index.shape[1]),
        lambda: screen_of(index, omega, levels_ref[:1], mean),
        tables,
    )


def odd_second_kernel(state_in_ref, plane_ref, image_in_ref, *refs):
    constants, (state_ref, image_ref) = refs[: 2 + TABLES], refs[2 + TABLES :]
    rows = image_ref.shape[0]

    @pl.when(is_odd())
    def _():
        planes, image = step_from(state_in_ref, plane_ref, constants)
        store_planes(state_ref, planes)
        for start in range(4 * rows, state_ref.shape[0], EXTRA):
            state_ref[start : start + EXTRA] = state_in_ref[4 * rows :]
        image_ref[...] = image_in_ref[...] + image

    @pl.when(is_even())
    def _():
        image_ref[...] = image_in_ref[...]


def odd_ahead_kernel(state_in_ref, plane_ref, *refs):
    constants, (image_ref,) = refs[: 2 + TABLES], refs[2 + TABLES :]
    has_next = is_odd() & (lax.axis_index("slab") < lax.axis_size("slab") - 1)

    @pl.when(has_next)
    def _():
        _, image = step_from(state_in_ref, plane_ref, constants)
        image_ref[...] = image

    @pl.when(jnp.logical_not(has_next))
    def _():
        image_ref[...] = jnp.zeros_like(image_ref)


def fill_wide(ref, raw):
    rows = raw.shape[0]
    ref[:rows] = raw
    ref[rows:] = jnp.zeros((ref.shape[0] - rows, ref.shape[1]), jnp.float32)


def even_arrival_kernel(state_in_ref, plane_ref, image_in_ref, *refs):
    constants, (state_ref, image_ref, up_ref) = refs[: 2 + TABLES], refs[2 + TABLES :]
    rows = image_ref.shape[0]

    @pl.when(is_even())
    def _():
        planes, image = step_from(state_in_ref, plane_ref, constants)
        store_planes(state_ref, planes)
        state_ref[4 * rows :] = state_in_ref[4 * rows : 4 * rows + EXTRA]
        image = image_in_ref[...] + image
        image_ref[...] = image
        fill_wide(up_ref, image)

    @pl.when(is_odd())
    def _():
        image_ref[...] = image_in_ref[...]


def odd_last_kernel(state_in_ref, plane_ref, image_in_ref, ahead_ref, *refs):
    constants, (state_ref, raw_ref, base_ref) = refs[: 2 + TABLES], refs[2 + TABLES :]

    @pl.when(is_odd())
    def _():
        planes, image = step_from(state_in_ref, plane_ref, constants)
        store_planes(state_ref, planes)
        raw = image_in_ref[...] + image
        fill_wide(raw_ref, raw)
        base_ref[...] = raw - 0.25 * ahead_ref[...]


def even_last_kernel(
    state_in_ref, plane_ref, image_in_ref, odd_raw_ref, odd_base_ref, *refs
):
    constants, (state_ref, raw_ref, base_ref) = refs[: 2 + TABLES], refs[2 + TABLES :]

    @pl.when(is_even())
    def _():
        planes, image = step_from(state_in_ref, plane_ref, constants)
        store_planes(state_ref, planes)
        raw = image_in_ref[...] + image
        raw_ref[...] = raw
        base_ref[...] = raw

    @pl.when(is_odd())
    def _():
        raw_ref[...] = odd_raw_ref[: raw_ref.shape[0]]
        base_ref[...] = odd_base_ref[...]


def write_kernel(odd_ref, even_ref, fields_hbm, done_ref, sems):
    rows = even_ref.shape[0] // 4

    def write(ref):
        copies = [
            pltpu.make_async_copy(
                ref.at[pl.ds(i * rows, rows)], fields_hbm.at[0, i // 2, i % 2], sems.at[i]
            )
            for i in range(4)
        ]
        for copy in copies:
            copy.start()
        for copy in copies:
            copy.wait()

    pl.when(is_odd())(functools.partial(write, odd_ref))
    pl.when(is_even())(functools.partial(write, even_ref))
    done_ref[...] = jnp.zeros_like(done_ref)


def stencil_kernel(base_ref, below_ref, above_ref, swap_ref, done_ref, image_ref):
    del done_ref
    rows = base_ref.shape[0]
    off = below_ref[:rows] + above_ref[:rows]
    image_ref[0] = base_ref[...] - 0.25 * (swap_ref[...] + off)


def body(fields, freq_index, slowness_index, slowness_table):
    rows, cols = slowness_index.shape[1:]
    slabs = lax.axis_size("slab")
    on_pairs = [(i, i + 1) for i in range(0, slabs - 1, 2)]
    off_pairs = [(i, i + 1) for i in range(1, slabs - 1, 2)]
    on_back = [(j, i) for i, j in on_pairs]
    off_back = [(j, i) for i, j in off_pairs]

    f32 = jnp.float32
    vmem = pl.BlockSpec(memory_space=pltpu.VMEM)
    hbm = pl.BlockSpec(memory_space=pltpu.HBM)
    products = 24 * (2 * rows) * cols * cols
    cost = pl.CostEstimate(flops=2 * products, bytes_accessed=16 * rows * cols * 4, transcendentals=0)

    long = pl.CostEstimate(
        flops=10 * 2 * products, bytes_accessed=10 * 16 * rows * cols * 4, transcendentals=0
    )

    def shape_of(height):
        return jax.ShapeDtypeStruct((height, cols), f32)

    def call(kernel, name, operands, out_shapes, cost=cost, **rest):
        rest.setdefault("in_specs", [vmem] * len(operands))
        rest.setdefault("out_specs", (vmem,) * len(out_shapes))
        return pl.pallas_call(
            kernel,
            out_shape=tuple(out_shapes),
            compiler_params=pltpu.CompilerParams(vmem_limit_bytes=32 * 1024 * 1024),
            cost_estimate=cost,
            name=name,
            **rest,
        )(*operands)

    long_state_shape = shape_of(4 * rows + 2 * EXTRA)
    state_shape, plane_shape, image_shape = shape_of(4 * rows + EXTRA), shape_of(rows + EXTRA), shape_of(rows)
    tables = [jnp.asarray(table) for table in dft_tables(rows, cols)]
    table_shapes = [jax.ShapeDtypeStruct(t.shape, t.dtype) for t in tables]
    levels_shape = jax.ShapeDtypeStruct((EXTRA,) + slowness_table.shape, f32)
    kept_shapes = [plane_shape, image_shape, shape_of(rows // 2 + EXTRA), levels_shape] + table_shapes
    loaded = (fields, slowness_index, slowness_table[None], *tables)
    operands = (freq_index,) + tuple(
        pltpu.with_memory_space_constraint(x, pltpu.HBM) for x in loaded
    )
    scratch = [
        pltpu.SMEM(freq_index.shape, freq_index.dtype),
        pltpu.VMEM(fields.shape, f32),
        pltpu.VMEM(slowness_index.shape, slowness_index.dtype),
        pltpu.VMEM((1,) + slowness_table.shape, f32),
        pltpu.SemaphoreType.DMA((4 + TABLES,)),
    ]
    odd_state, *kept = call(
        odd_first_kernel, "odd_first_step", operands, [long_state_shape] + kept_shapes,
        in_specs=[hbm] * len(operands), scratch_shapes=scratch,
    )
    from_off = lax.ppermute(odd_state, "slab", off_pairs)
    even_state, plane, image, *constants = call(
        even_first_kernel, "even_first_step", (*operands, *kept), [state_shape] + kept_shapes,
        in_specs=[hbm] * len(operands) + [vmem] * len(kept), scratch_shapes=scratch,
    )
    from_on = lax.ppermute(even_state, "slab", on_pairs)
    next_plane = lax.ppermute(plane, "slab", off_back)
    odd_state, image = call(
        odd_second_kernel, "odd_second_step", (from_on, plane, image, *constants),
        [shape_of(4 * rows + 3 * EXTRA), image_shape], cost=None,
    )
    last_off = lax.ppermute(odd_state, "slab", off_pairs)
    even_state, image, up_image = call(
        even_arrival_kernel, "even_arrival_step", (from_off, plane, image, *constants),
        [state_shape, image_shape, shape_of(rows + 2 * EXTRA)],
    )
    last_on = lax.ppermute(even_state, "slab", on_pairs)
    below = lax.ppermute(up_image, "slab", off_back)
    (ahead,) = call(
        odd_ahead_kernel, "odd_step_ahead", (odd_state, next_plane, *constants), [image_shape],
        cost=long,
    )
    odd_fields, odd_raw, odd_base = call(
        odd_last_kernel, "odd_last_step", (last_on, plane, image, ahead, *constants),
        [shape_of(4 * rows), shape_of(rows + EXTRA), image_shape], cost=None,
    )
    above = lax.ppermute(odd_raw, "slab", off_pairs)
    even_fields, raw, base = call(
        even_last_kernel, "even_last_step",
        (last_off, plane, image, odd_raw, odd_base, *constants),
        [shape_of(4 * rows), image_shape, image_shape], cost=None,
    )
    swapped = lax.ppermute(raw, "slab", on_pairs + on_back)
    fields_out, done = call(
        write_kernel, "write_fields", (odd_fields, even_fields),
        [jax.ShapeDtypeStruct(fields.shape, f32), jax.ShapeDtypeStruct((EXTRA, LANES), f32)],
        out_specs=(hbm, vmem), scratch_shapes=[pltpu.SemaphoreType.DMA((4,))], cost=None,
    )
    (image,) = call(
        stencil_kernel, "image_stencil", (base, below, above, swapped, done),
        [jax.ShapeDtypeStruct((1, rows, cols), f32)], cost=None,
    )
    return image, fields_out


def solution(mesh):
    return jax.shard_map(
        body,
        mesh=mesh,
        in_specs=(
            P(("shots", "slab"), None, None, None, None),
            P(("shots", "slab")),
            P("slab", None, None),
            P(),
        ),
        out_specs=(P(("shots", "slab"), None, None), P(("shots", "slab"), None, None, None, None)),
        check_vma=False,
    )
```

```python
import functools
import math

import jax
import jax.numpy as jnp
import ml_dtypes
import numpy as np
from jax import lax
from jax.experimental import pallas as pl
from jax.experimental.pallas import tpu as pltpu
from jax.sharding import PartitionSpec as P

TICKS = 3
NFREQ = 512
EXTRA = 8
LANES = 128
TABLES = 2
TWO_PI = 2.0 * math.pi


def split_table(angle):
    parts = np.concatenate([np.cos(angle), np.sin(angle)], axis=0)
    high = parts.astype(np.float32).astype(ml_dtypes.bfloat16)
    low = (parts - high.astype(np.float64)).astype(np.float32).astype(ml_dtypes.bfloat16)
    return np.concatenate([high, low], axis=0)


def x_order(rows):
    front = np.arange(rows // 2)
    return np.concatenate([front, [rows // 2], rows - front[1:]])


def dft_tables(rows, cols):
    x_no, y_no = np.arange(rows), np.arange(cols // 2)
    to_x = np.outer(x_order(rows), x_no) % rows * (TWO_PI / rows)
    even = np.outer(y_no, 2 * y_no) % cols * (TWO_PI / cols)
    to_odd = np.outer(y_no, 2 * y_no + 1) % cols * (TWO_PI / cols)
    groups = ((to_x, to_x.T), (even, to_odd, to_odd.T))
    return [np.concatenate([split_table(angle) for angle in group]) for group in groups]


def table_views(x_ref, y_ref):
    views = []
    for ref, count in ((x_ref, 2), (y_ref, 3)):
        size = 4 * ref.shape[1]
        views += [ref.at[pl.ds(i * size, size)] for i in range(count)]
    return views


def halves(value):
    high = value.astype(jnp.bfloat16)
    return high, (value - high.astype(jnp.float32)).astype(jnp.bfloat16)


def dot(left, right):
    return jnp.dot(left, right, preferred_element_type=jnp.float32)


def table_parts(table_ref, turn):
    size = table_ref.shape[1]
    parts = []
    for start in (0, 2 * size):
        cos = table_ref[start : start + size]
        sin = table_ref[start + size : start + 2 * size]
        if turn:
            parts.append(stack(side(cos, sin), side(-sin, cos)))
        else:
            parts.append(stack(side(cos, -sin), side(sin, cos)))
    return parts


def dot_right(value, table_ref):
    table_high, table_low = table_parts(table_ref, False)
    high, low = halves(value)
    both = dot(stack(high, low), table_high)
    rows = value.shape[0]
    return both[:rows] + (both[rows:] + dot(high, table_low))


def dot_left(table_ref, value):
    table_high, table_low = table_parts(table_ref, True)
    high, low = halves(value)
    both = dot(stack(table_high, table_low), high)
    rows = table_high.shape[0]
    return both[:rows] + (both[rows:] + dot(table_high, low))


def cos_sin(angle):
    turns = jnp.floor(angle * (1.0 / math.pi) + 0.5)
    pairs = turns * 0.5
    flip = 1.0 - 4.0 * (pairs - jnp.floor(pairs))
    rest = angle - turns * math.pi
    sq = rest * rest
    sin = -1.98089830e-4 + sq * 2.60501962e-6
    sin = 8.33304978e-3 + sq * sin
    sin = -1.66666579e-1 + sq * sin
    sin = 9.99999996e-1 + sq * sin
    cos = -1.38535979e-3 + sq * 2.31515763e-5
    cos = 4.16635698e-2 + sq * cos
    cos = -4.99999047e-1 + sq * cos
    cos = 9.99999953e-1 + sq * cos
    return cos * flip, sin * (rest * flip)


def wave_square(rows, cols):
    half = cols // 2
    shape = (rows // 2 + EXTRA, cols)
    row = lax.broadcasted_iota(jnp.int32, shape, 0)
    row = jnp.where(row > rows // 2, rows // 2 - row, row)
    col = lax.broadcasted_iota(jnp.int32, shape, 1)
    col = jnp.where(col < half, 2 * col, 2 * (col - half) + 1)
    col = jnp.where(col < half, col, col - cols)
    wave_x = row.astype(jnp.float32) * (TWO_PI / rows)
    wave_y = col.astype(jnp.float32) * (TWO_PI / cols)
    return wave_x * wave_x + wave_y * wave_y


def depth_factor(omega_mean, wave_sq, rows, cols):
    gap = omega_mean * omega_mean - wave_sq
    root = jnp.sqrt(jnp.abs(gap))
    cos, sin = cos_sin(root)
    scale = 1.0 / (rows * cols)
    wave = gap > 0.0
    cos = jnp.where(wave, cos, jnp.exp(-root)) * scale
    sin = jnp.where(wave, sin, 0.0) * scale
    return [stack(part, part[EXTRA : rows // 2]) for part in (cos, sin)]


def side(*parts):
    return jnp.concatenate(parts, axis=1)


def stack(*parts):
    return jnp.concatenate(parts, axis=0)


def depth_step(fields, factor, screen, tables):
    left, left_back, even, odd, odd_back = table_views(*tables)
    spectra = []
    for real, imag in fields:
        half = real.shape[1] // 2
        first = side(real[:, :half], imag[:, :half])
        second = side(real[:, half:], imag[:, half:])
        spectra.append((dot_right(first + second, even), dot_right(first - second, odd)))
    spectra = [
        stack(side(low[:, :half], high[:, :half]), side(low[:, half:], high[:, half:]))
        for low, high in spectra
    ]
    spectra = [dot_left(left, spectrum) for spectrum in spectra]
    cos, sin = factor()
    rows = cos.shape[0]
    moved = []
    for spectrum in spectra:
        real, imag = spectrum[:rows], spectrum[rows:]
        moved.append(stack(real * sin + imag * cos, real * cos - imag * sin))
    backs = [dot_left(left_back, spectrum) for spectrum in moved]
    parts = []
    for back in backs:
        sum_part = dot_right(side(back[:rows, :half], back[rows:, :half]), even)
        gap_part = dot_right(side(back[:rows, half:], back[rows:, half:]), odd_back)
        parts.append((sum_part, gap_part))
    cos, sin = screen()
    results = []
    for sum_part, gap_part in parts:
        first, second = sum_part + gap_part, sum_part - gap_part
        real = side(first[:, half:], second[:, half:])
        imag = side(first[:, :half], second[:, :half])
        results.append((real * cos - imag * sin, real * sin + imag * cos))
    return results


def both_fields(state_ref, rows, factor, screen, tables):
    def fields():
        if len(state_ref.shape) == 2:
            parts = [state_ref[i * rows : (i + 1) * rows] for i in range(4)]
        else:
            parts = [state_ref[0, i, j] for i in range(2) for j in range(2)]
        s_real, s_imag, r_real, r_imag = parts
        return (s_real, s_imag), (r_imag, r_real)

    (s_real, s_imag), (r_imag, r_real) = depth_step(fields(), factor, screen, tables)
    return (s_real, s_imag, r_real, r_imag), s_real * r_real + s_imag * r_imag


def look_up(index, *tables):
    found = []
    for table in tables:
        pieces = []
        for start in range(0, index.shape[1], LANES):
            piece = index[:, start : start + LANES]
            value = jnp.zeros(piece.shape, jnp.float32)
            for low in range(0, table.shape[1], LANES):
                entries = jnp.broadcast_to(table[:, low : low + LANES], piece.shape)
                inside = jnp.clip(piece - low, 0, LANES - 1)
                picked = jnp.take_along_axis(entries, inside, axis=1)
                value = jnp.where(piece >= low, picked, value)
            pieces.append(value)
        found.append(side(*pieces))
    return found


def screen_of(index, omega, entries, mean):
    return look_up(index, *cos_sin(omega * (entries - mean)))


def store_planes(ref, planes):
    rows = planes[0].shape[0]
    for i, plane in enumerate(planes):
        ref[i * rows : (i + 1) * rows] = plane


def is_odd():
    return lax.rem(lax.axis_index("slab"), 2) == 1


def is_even():
    return jnp.logical_not(is_odd())


def load_and_step(operands, outputs, scratch):
    freq_hbm, fields_hbm, index_hbm, entries_hbm, *tables_hbm = operands
    state_ref, plane_ref, image_ref, wave_ref, levels_ref, *tables = outputs
    freq_ref, own_ref, index_ref, entries_ref, sems = scratch
    rows, cols = image_ref.shape
    pairs = [(fields_hbm, own_ref), (index_hbm, index_ref), (entries_hbm, entries_ref)]
    pairs += [(freq_hbm, freq_ref), *zip(tables_hbm, tables)]
    copies = [pltpu.make_async_copy(*pair, sems.at[i]) for i, pair in enumerate(pairs)]
    for copy in copies:
        copy.start()
    wave_sq = wave_square(rows, cols)
    wave_ref[...] = wave_sq
    for copy in copies:
        copy.wait()
    index, entries = index_ref[0], entries_ref[...]
    omega = 1.0 + freq_ref[0].astype(jnp.float32) * (1.0 / NFREQ)
    means = []

    def factor():
        (slow,) = look_up(index, entries)
        means.append(jnp.sum(slow, axis=(0, 1), keepdims=True) * (1.0 / (rows * cols)))
        return depth_factor(omega * means[0], wave_sq, rows, cols)

    planes, image = both_fields(
        own_ref, rows, factor, lambda: screen_of(index, omega, entries, means[0]), tables
    )
    store_planes(state_ref, planes)
    state_ref[4 * rows :] = jnp.full((state_ref.shape[0] - 4 * rows, cols), omega, jnp.float32)
    image_ref[...] = image
    plane_ref[:rows] = index.astype(jnp.float32)
    plane_ref[rows:] = jnp.broadcast_to(means[0], (EXTRA, cols))
    levels_ref[...] = jnp.broadcast_to(entries, levels_ref.shape)


def odd_first_kernel(*refs):
    operands, refs = refs[: 4 + TABLES], refs[4 + TABLES :]
    outputs, scratch = refs[: 5 + TABLES], refs[5 + TABLES :]
    pl.when(is_odd())(functools.partial(load_and_step, operands, outputs, scratch))


def even_first_kernel(*refs):
    operands, refs = refs[: 4 + TABLES], refs[5 + TABLES :]
    outputs, scratch = refs[: 5 + TABLES], refs[5 + TABLES :]
    pl.when(is_even())(functools.partial(load_and_step, operands, outputs, scratch))


def step_from(state_ref, plane_ref, constants):
    wave_ref, levels_ref, *tables = constants
    rows = plane_ref.shape[0] - EXTRA
    omega = state_ref[4 * rows : 4 * rows + 1, :1]
    mean = plane_ref[rows : rows + 1, :1]
    index = plane_ref[:rows].astype(jnp.int32)
    return both_fields(
        state_ref,
        rows,
        lambda: depth_factor(omega * mean, wave_ref[...], rows, index.shape[1]),
        lambda: screen_of(index, omega, levels_ref[:1], mean),
        tables,
    )


def odd_second_kernel(state_in_ref, plane_ref, image_in_ref, *refs):
    constants, (state_ref, image_ref) = refs[: 2 + TABLES], refs[2 + TABLES :]
    rows = image_ref.shape[0]

    @pl.when(is_odd())
    def _():
        planes, image = step_from(state_in_ref, plane_ref, constants)
        store_planes(state_ref, planes)
        for start in range(4 * rows, state_ref.shape[0], EXTRA):
            state_ref[start : start + EXTRA] = state_in_ref[4 * rows :]
        image_ref[...] = image_in_ref[...] + image


def odd_ahead_kernel(state_in_ref, plane_ref, *refs):
    constants, (image_ref,) = refs[: 2 + TABLES], refs[2 + TABLES :]
    has_next = is_odd() & (lax.axis_index("slab") < lax.axis_size("slab") - 1)

    @pl.when(has_next)
    def _():
        _, image = step_from(state_in_ref, plane_ref, constants)
        image_ref[...] = image

    @pl.when(jnp.logical_not(has_next))
    def _():
        image_ref[...] = jnp.zeros_like(image_ref)


def fill_wide(ref, raw):
    rows = raw.shape[0]
    ref[:rows] = raw
    ref[rows:] = jnp.zeros((ref.shape[0] - rows, ref.shape[1]), jnp.float32)


def even_arrival_kernel(state_in_ref, plane_ref, image_in_ref, *refs):
    constants, (state_ref, image_ref, up_ref) = refs[: 2 + TABLES], refs[2 + TABLES :]
    rows = image_ref.shape[0]

    @pl.when(is_even())
    def _():
        planes, image = step_from(state_in_ref, plane_ref, constants)
        store_planes(state_ref, planes)
        state_ref[4 * rows :] = state_in_ref[4 * rows : 4 * rows + EXTRA]
        image = image_in_ref[...] + image
        image_ref[...] = image
        fill_wide(up_ref, image)


def odd_last_kernel(state_in_ref, plane_ref, image_in_ref, ahead_ref, *refs):
    constants, (state_ref, raw_ref, base_ref) = refs[: 2 + TABLES], refs[2 + TABLES :]

    @pl.when(is_odd())
    def _():
        planes, image = step_from(state_in_ref, plane_ref, constants)
        store_planes(state_ref, planes)
        raw = image_in_ref[...] + image
        fill_wide(raw_ref, raw)
        base_ref[...] = raw - 0.25 * ahead_ref[...]


def even_last_kernel(
    state_in_ref, plane_ref, image_in_ref, odd_raw_ref, odd_base_ref, *refs
):
    constants, (state_ref, raw_ref, base_ref) = refs[: 2 + TABLES], refs[2 + TABLES :]

    @pl.when(is_even())
    def _():
        planes, image = step_from(state_in_ref, plane_ref, constants)
        store_planes(state_ref, planes)
        raw = image_in_ref[...] + image
        raw_ref[...] = raw
        base_ref[...] = raw

    @pl.when(is_odd())
    def _():
        raw_ref[...] = odd_raw_ref[: raw_ref.shape[0]]
        base_ref[...] = odd_base_ref[...]


def write_kernel(odd_ref, even_ref, fields_hbm, done_ref, sems):
    rows = even_ref.shape[0] // 4

    def write(ref):
        copies = [
            pltpu.make_async_copy(
                ref.at[pl.ds(i * rows, rows)], fields_hbm.at[0, i // 2, i % 2], sems.at[i]
            )
            for i in range(4)
        ]
        for copy in copies:
            copy.start()
        for copy in copies:
            copy.wait()

    pl.when(is_odd())(functools.partial(write, odd_ref))
    pl.when(is_even())(functools.partial(write, even_ref))
    done_ref[...] = jnp.zeros_like(done_ref)


def stencil_kernel(base_ref, below_ref, above_ref, swap_ref, done_ref, image_ref):
    del done_ref
    rows = base_ref.shape[0]
    off = below_ref[:rows] + above_ref[:rows]
    image_ref[0] = base_ref[...] - 0.25 * (swap_ref[...] + off)


def body(fields, freq_index, slowness_index, slowness_table):
    rows, cols = slowness_index.shape[1:]
    slabs = lax.axis_size("slab")
    on_pairs = [(i, i + 1) for i in range(0, slabs - 1, 2)]
    off_pairs = [(i, i + 1) for i in range(1, slabs - 1, 2)]
    on_back = [(j, i) for i, j in on_pairs]
    off_back = [(j, i) for i, j in off_pairs]

    f32 = jnp.float32
    vmem = pl.BlockSpec(memory_space=pltpu.VMEM)
    hbm = pl.BlockSpec(memory_space=pltpu.HBM)
    products = 24 * (2 * rows) * cols * cols
    cost = pl.CostEstimate(flops=2 * products, bytes_accessed=16 * rows * cols * 4, transcendentals=0)

    long = pl.CostEstimate(
        flops=13 * products, bytes_accessed=104 * rows * cols * 4, transcendentals=0
    )

    def shape_of(height):
        return jax.ShapeDtypeStruct((height, cols), f32)

    def call(kernel, name, operands, out_shapes, cost=cost, **rest):
        rest.setdefault("in_specs", [vmem] * len(operands))
        rest.setdefault("out_specs", (vmem,) * len(out_shapes))
        return pl.pallas_call(
            kernel,
            out_shape=tuple(out_shapes),
            compiler_params=pltpu.CompilerParams(vmem_limit_bytes=32 * 1024 * 1024),
            cost_estimate=cost,
            name=name,
            **rest,
        )(*operands)

    long_state_shape = shape_of(4 * rows + 2 * EXTRA)
    state_shape, plane_shape, image_shape = shape_of(4 * rows + EXTRA), shape_of(rows + EXTRA), shape_of(rows)
    tables = [jnp.asarray(table) for table in dft_tables(rows, cols)]
    table_shapes = [jax.ShapeDtypeStruct(t.shape, t.dtype) for t in tables]
    levels_shape = jax.ShapeDtypeStruct((EXTRA,) + slowness_table.shape, f32)
    kept_shapes = [plane_shape, image_shape, shape_of(rows // 2 + EXTRA), levels_shape] + table_shapes
    loaded = (fields, slowness_index, slowness_table[None], *tables)
    operands = (freq_index,) + tuple(
        pltpu.with_memory_space_constraint(x, pltpu.HBM) for x in loaded
    )
    scratch = [
        pltpu.SMEM(freq_index.shape, freq_index.dtype),
        pltpu.VMEM(fields.shape, f32),
        pltpu.VMEM(slowness_index.shape, slowness_index.dtype),
        pltpu.VMEM((1,) + slowness_table.shape, f32),
        pltpu.SemaphoreType.DMA((4 + TABLES,)),
    ]
    odd_state, odd_plane, odd_image, *odd_constants = call(
        odd_first_kernel, "odd_first_step", operands, [long_state_shape] + kept_shapes,
        in_specs=[hbm] * len(operands), scratch_shapes=scratch,
    )
    from_off = lax.ppermute(odd_state, "slab", off_pairs)
    even_state, even_plane, even_image, *even_constants = call(
        even_first_kernel, "even_first_step", (*operands, odd_image), [state_shape] + kept_shapes,
        in_specs=[hbm] * len(operands) + [vmem], scratch_shapes=scratch,
    )
    from_on = lax.ppermute(even_state, "slab", on_pairs)
    next_plane = lax.ppermute(even_plane, "slab", off_back)
    odd_state, odd_image = call(
        odd_second_kernel, "odd_second_step", (from_on, odd_plane, odd_image, *odd_constants),
        [shape_of(4 * rows + 3 * EXTRA), image_shape], cost=None,
    )
    last_off = lax.ppermute(odd_state, "slab", off_pairs)
    even_state, even_image, up_image = call(
        even_arrival_kernel, "even_arrival_step", (from_off, even_plane, even_image, *even_constants),
        [state_shape, image_shape, shape_of(rows + 2 * EXTRA)],
    )
    last_on = lax.ppermute(even_state, "slab", on_pairs)
    below = lax.ppermute(up_image, "slab", off_back)
    (ahead,) = call(
        odd_ahead_kernel, "odd_step_ahead", (odd_state, next_plane, *odd_constants), [image_shape],
        cost=long,
    )
    odd_fields, odd_raw, odd_base = call(
        odd_last_kernel, "odd_last_step", (last_on, odd_plane, odd_image, ahead, *odd_constants),
        [shape_of(4 * rows), shape_of(rows + EXTRA), image_shape], cost=None,
    )
    above = lax.ppermute(odd_raw, "slab", off_pairs)
    even_fields, raw, base = call(
        even_last_kernel, "even_last_step",
        (last_off, even_plane, even_image, odd_raw, odd_base, *even_constants),
        [shape_of(4 * rows), image_shape, image_shape], cost=None,
    )
    swapped = lax.ppermute(raw, "slab", on_pairs + on_back)
    fields_out, done = call(
        write_kernel, "write_fields", (odd_fields, even_fields),
        [jax.ShapeDtypeStruct(fields.shape, f32), jax.ShapeDtypeStruct((EXTRA, LANES), f32)],
        out_specs=(hbm, vmem), scratch_shapes=[pltpu.SemaphoreType.DMA((4,))], cost=None,
    )
    (image,) = call(
        stencil_kernel, "image_stencil", (base, below, above, swapped, done),
        [jax.ShapeDtypeStruct((1, rows, cols), f32)], cost=None,
    )
    return image, fields_out


def solution(mesh):
    return jax.shard_map(
        body,
        mesh=mesh,
        in_specs=(
            P(("shots", "slab"), None, None, None, None),
            P(("shots", "slab")),
            P("slab", None, None),
            P(),
        ),
        out_specs=(P(("shots", "slab"), None, None), P(("shots", "slab"), None, None, None, None)),
        check_vma=False,
    )
```

```python
import functools
import math

import jax
import jax.numpy as jnp
import ml_dtypes
import numpy as np
from jax import lax
from jax.experimental import pallas as pl
from jax.experimental.pallas import tpu as pltpu
from jax.sharding import PartitionSpec as P

TICKS = 3
NFREQ = 512
EXTRA = 8
LANES = 128
TABLES = 2
TWO_PI = 2.0 * math.pi


def split_table(angle):
    parts = np.concatenate([np.cos(angle), np.sin(angle)], axis=0)
    high = parts.astype(np.float32).astype(ml_dtypes.bfloat16)
    low = (parts - high.astype(np.float64)).astype(np.float32).astype(ml_dtypes.bfloat16)
    return np.concatenate([high, low], axis=0)


def x_order(rows):
    front = np.arange(rows // 2)
    return np.concatenate([front, [rows // 2], rows - front[1:]])


def dft_tables(rows, cols):
    x_no, y_no = np.arange(rows), np.arange(cols // 2)
    to_x = np.outer(x_order(rows), x_no) % rows * (TWO_PI / rows)
    even = np.outer(y_no, 2 * y_no) % cols * (TWO_PI / cols)
    to_odd = np.outer(y_no, 2 * y_no + 1) % cols * (TWO_PI / cols)
    groups = ((to_x, to_x.T), (even, to_odd, to_odd.T))
    return [np.concatenate([split_table(angle) for angle in group]) for group in groups]


def table_views(x_ref, y_ref):
    views = []
    for ref, count in ((x_ref, 2), (y_ref, 3)):
        size = 4 * ref.shape[1]
        views += [ref.at[pl.ds(i * size, size)] for i in range(count)]
    return views


def halves(value):
    high = value.astype(jnp.bfloat16)
    return high, (value - high.astype(jnp.float32)).astype(jnp.bfloat16)


def dot(left, right):
    return jnp.dot(left, right, preferred_element_type=jnp.float32)


def table_parts(table_ref, turn):
    size = table_ref.shape[1]
    parts = []
    for start in (0, 2 * size):
        cos = table_ref[start : start + size]
        sin = table_ref[start + size : start + 2 * size]
        if turn:
            parts.append(stack(side(cos, sin), side(-sin, cos)))
        else:
            parts.append(stack(side(cos, -sin), side(sin, cos)))
    return parts


def dot_right(value, table_ref):
    table_high, table_low = table_parts(table_ref, False)
    high, low = halves(value)
    return dot(side(high, low, high), stack(table_high, table_high, table_low))


def dot_left(table_ref, value):
    table_high, table_low = table_parts(table_ref, True)
    high, low = halves(value)
    both = dot(stack(table_high, table_low), high)
    rows = table_high.shape[0]
    return both[:rows] + (both[rows:] + dot(table_high, low))


def cos_sin(angle):
    turns = jnp.floor(angle * (1.0 / math.pi) + 0.5)
    pairs = turns * 0.5
    flip = 1.0 - 4.0 * (pairs - jnp.floor(pairs))
    rest = angle - turns * math.pi
    sq = rest * rest
    sin = -1.98089830e-4 + sq * 2.60501962e-6
    sin = 8.33304978e-3 + sq * sin
    sin = -1.66666579e-1 + sq * sin
    sin = 9.99999996e-1 + sq * sin
    cos = -1.38535979e-3 + sq * 2.31515763e-5
    cos = 4.16635698e-2 + sq * cos
    cos = -4.99999047e-1 + sq * cos
    cos = 9.99999953e-1 + sq * cos
    return cos * flip, sin * (rest * flip)


def wave_square(rows, cols):
    half = cols // 2
    shape = (rows // 2 + EXTRA, cols)
    row = lax.broadcasted_iota(jnp.int32, shape, 0)
    row = jnp.where(row > rows // 2, rows // 2 - row, row)
    col = lax.broadcasted_iota(jnp.int32, shape, 1)
    col = jnp.where(col < half, 2 * col, 2 * (col - half) + 1)
    col = jnp.where(col < half, col, col - cols)
    wave_x = row.astype(jnp.float32) * (TWO_PI / rows)
    wave_y = col.astype(jnp.float32) * (TWO_PI / cols)
    return wave_x * wave_x + wave_y * wave_y


def depth_factor(omega_mean, wave_sq, rows, cols):
    gap = omega_mean * omega_mean - wave_sq
    root = jnp.sqrt(jnp.abs(gap))
    cos, sin = cos_sin(root)
    scale = 1.0 / (rows * cols)
    wave = gap > 0.0
    cos = jnp.where(wave, cos, jnp.exp(-root)) * scale
    sin = jnp.where(wave, sin, 0.0) * scale
    return [stack(part, part[EXTRA : rows // 2]) for part in (cos, sin)]


def side(*parts):
    return jnp.concatenate(parts, axis=1)


def stack(*parts):
    return jnp.concatenate(parts, axis=0)


def depth_step(fields, factor, screen, tables):
    left, left_back, even, odd, odd_back = table_views(*tables)
    spectra = []
    for real, imag in fields:
        half = real.shape[1] // 2
        first = side(real[:, :half], imag[:, :half])
        second = side(real[:, half:], imag[:, half:])
        spectra.append((dot_right(first + second, even), dot_right(first - second, odd)))
    spectra = [
        stack(side(low[:, :half], high[:, :half]), side(low[:, half:], high[:, half:]))
        for low, high in spectra
    ]
    spectra = [dot_left(left, spectrum) for spectrum in spectra]
    cos, sin = factor()
    rows = cos.shape[0]
    moved = []
    for spectrum in spectra:
        real, imag = spectrum[:rows], spectrum[rows:]
        moved.append(stack(real * sin + imag * cos, real * cos - imag * sin))
    backs = [dot_left(left_back, spectrum) for spectrum in moved]
    parts = []
    for back in backs:
        sum_part = dot_right(side(back[:rows, :half], back[rows:, :half]), even)
        gap_part = dot_right(side(back[:rows, half:], back[rows:, half:]), odd_back)
        parts.append((sum_part, gap_part))
    cos, sin = screen()
    results = []
    for sum_part, gap_part in parts:
        first, second = sum_part + gap_part, sum_part - gap_part
        real = side(first[:, half:], second[:, half:])
        imag = side(first[:, :half], second[:, :half])
        results.append((real * cos - imag * sin, real * sin + imag * cos))
    return results


def both_fields(state_ref, rows, factor, screen, tables):
    def fields():
        if len(state_ref.shape) == 2:
            parts = [state_ref[i * rows : (i + 1) * rows] for i in range(4)]
        else:
            parts = [state_ref[0, i, j] for i in range(2) for j in range(2)]
        s_real, s_imag, r_real, r_imag = parts
        return (s_real, s_imag), (r_imag, r_real)

    (s_real, s_imag), (r_imag, r_real) = depth_step(fields(), factor, screen, tables)
    return (s_real, s_imag, r_real, r_imag), s_real * r_real + s_imag * r_imag


def look_up(index, *tables):
    found = []
    for table in tables:
        pieces = []
        for start in range(0, index.shape[1], LANES):
            piece = index[:, start : start + LANES]
            value = jnp.zeros(piece.shape, jnp.float32)
            for low in range(0, table.shape[1], LANES):
                entries = jnp.broadcast_to(table[:, low : low + LANES], piece.shape)
                inside = jnp.clip(piece - low, 0, LANES - 1)
                picked = jnp.take_along_axis(entries, inside, axis=1)
                value = jnp.where(piece >= low, picked, value)
            pieces.append(value)
        found.append(side(*pieces))
    return found


def screen_of(index, omega, entries, mean):
    return look_up(index, *cos_sin(omega * (entries - mean)))


def store_planes(ref, planes):
    rows = planes[0].shape[0]
    for i, plane in enumerate(planes):
        ref[i * rows : (i + 1) * rows] = plane


def is_odd():
    return lax.rem(lax.axis_index("slab"), 2) == 1


def is_even():
    return jnp.logical_not(is_odd())


def load_and_step(operands, outputs, scratch):
    freq_hbm, fields_hbm, index_hbm, entries_hbm, *tables_hbm = operands
    state_ref, plane_ref, image_ref, wave_ref, levels_ref, *tables = outputs
    freq_ref, own_ref, index_ref, entries_ref, sems = scratch
    rows, cols = image_ref.shape
    pairs = [(fields_hbm, own_ref), (index_hbm, index_ref), (entries_hbm, entries_ref)]
    pairs += [(freq_hbm, freq_ref), *zip(tables_hbm, tables)]
    copies = [pltpu.make_async_copy(*pair, sems.at[i]) for i, pair in enumerate(pairs)]
    for copy in copies:
        copy.start()
    wave_sq = wave_square(rows, cols)
    wave_ref[...] = wave_sq
    for copy in copies:
        copy.wait()
    index, entries = index_ref[0], entries_ref[...]
    omega = 1.0 + freq_ref[0].astype(jnp.float32) * (1.0 / NFREQ)
    means = []

    def factor():
        (slow,) = look_up(index, entries)
        means.append(jnp.sum(slow, axis=(0, 1), keepdims=True) * (1.0 / (rows * cols)))
        return depth_factor(omega * means[0], wave_sq, rows, cols)

    planes, image = both_fields(
        own_ref, rows, factor, lambda: screen_of(index, omega, entries, means[0]), tables
    )
    store_planes(state_ref, planes)
    state_ref[4 * rows :] = jnp.full((state_ref.shape[0] - 4 * rows, cols), omega, jnp.float32)
    image_ref[...] = image
    plane_ref[:rows] = index.astype(jnp.float32)
    plane_ref[rows:] = jnp.broadcast_to(means[0], (EXTRA, cols))
    levels_ref[...] = jnp.broadcast_to(entries, levels_ref.shape)


def odd_first_kernel(*refs):
    operands, refs = refs[: 4 + TABLES], refs[4 + TABLES :]
    outputs, scratch = refs[: 5 + TABLES], refs[5 + TABLES :]
    pl.when(is_odd())(functools.partial(load_and_step, operands, outputs, scratch))


def even_first_kernel(*refs):
    operands, refs = refs[: 4 + TABLES], refs[5 + TABLES :]
    outputs, scratch = refs[: 5 + TABLES], refs[5 + TABLES :]
    pl.when(is_even())(functools.partial(load_and_step, operands, outputs, scratch))


def step_from(state_ref, plane_ref, constants):
    wave_ref, levels_ref, *tables = constants
    rows = plane_ref.shape[0] - EXTRA
    omega = state_ref[4 * rows : 4 * rows + 1, :1]
    mean = plane_ref[rows : rows + 1, :1]
    index = plane_ref[:rows].astype(jnp.int32)
    return both_fields(
        state_ref,
        rows,
        lambda: depth_factor(omega * mean, wave_ref[...], rows, index.shape[1]),
        lambda: screen_of(index, omega, levels_ref[:1], mean),
        tables,
    )


def odd_second_kernel(state_in_ref, plane_ref, image_in_ref, *refs):
    constants, (state_ref, image_ref) = refs[: 2 + TABLES], refs[2 + TABLES :]
    rows = image_ref.shape[0]

    @pl.when(is_odd())
    def _():
        planes, image = step_from(state_in_ref, plane_ref, constants)
        store_planes(state_ref, planes)
        for start in range(4 * rows, state_ref.shape[0], EXTRA):
            state_ref[start : start + EXTRA] = state_in_ref[4 * rows :]
        image_ref[...] = image_in_ref[...] + image


def odd_ahead_kernel(state_in_ref, plane_ref, *refs):
    constants, (image_ref,) = refs[: 2 + TABLES], refs[2 + TABLES :]
    has_next = is_odd() & (lax.axis_index("slab") < lax.axis_size("slab") - 1)

    @pl.when(has_next)
    def _():
        _, image = step_from(state_in_ref, plane_ref, constants)
        image_ref[...] = image

    @pl.when(jnp.logical_not(has_next))
    def _():
        image_ref[...] = jnp.zeros_like(image_ref)


def fill_wide(ref, raw):
    rows = raw.shape[0]
    ref[:rows] = raw
    ref[rows:] = jnp.zeros((ref.shape[0] - rows, ref.shape[1]), jnp.float32)


def even_arrival_kernel(state_in_ref, plane_ref, image_in_ref, *refs):
    constants, (state_ref, image_ref, up_ref) = refs[: 2 + TABLES], refs[2 + TABLES :]
    rows = image_ref.shape[0]

    @pl.when(is_even())
    def _():
        planes, image = step_from(state_in_ref, plane_ref, constants)
        store_planes(state_ref, planes)
        state_ref[4 * rows :] = state_in_ref[4 * rows : 4 * rows + EXTRA]
        image = image_in_ref[...] + image
        image_ref[...] = image
        fill_wide(up_ref, image)


def odd_last_kernel(state_in_ref, plane_ref, image_in_ref, ahead_ref, *refs):
    constants, (state_ref, raw_ref, base_ref) = refs[: 2 + TABLES], refs[2 + TABLES :]

    @pl.when(is_odd())
    def _():
        planes, image = step_from(state_in_ref, plane_ref, constants)
        store_planes(state_ref, planes)
        raw = image_in_ref[...] + image
        fill_wide(raw_ref, raw)
        base_ref[...] = raw - 0.25 * ahead_ref[...]


def even_last_kernel(
    state_in_ref, plane_ref, image_in_ref, odd_raw_ref, odd_base_ref, *refs
):
    constants, (state_ref, raw_ref, base_ref) = refs[: 2 + TABLES], refs[2 + TABLES :]

    @pl.when(is_even())
    def _():
        planes, image = step_from(state_in_ref, plane_ref, constants)
        store_planes(state_ref, planes)
        raw = image_in_ref[...] + image
        raw_ref[...] = raw
        base_ref[...] = raw

    @pl.when(is_odd())
    def _():
        raw_ref[...] = odd_raw_ref[: raw_ref.shape[0]]
        base_ref[...] = odd_base_ref[...]


def write_kernel(odd_ref, even_ref, fields_hbm, done_ref, sems):
    rows = even_ref.shape[0] // 4

    def write(ref):
        copies = [
            pltpu.make_async_copy(
                ref.at[pl.ds(i * rows, rows)], fields_hbm.at[0, i // 2, i % 2], sems.at[i]
            )
            for i in range(4)
        ]
        for copy in copies:
            copy.start()
        for copy in copies:
            copy.wait()

    pl.when(is_odd())(functools.partial(write, odd_ref))
    pl.when(is_even())(functools.partial(write, even_ref))
    done_ref[...] = jnp.zeros_like(done_ref)


def stencil_kernel(base_ref, below_ref, above_ref, swap_ref, done_ref, image_ref):
    del done_ref
    rows = base_ref.shape[0]
    off = below_ref[:rows] + above_ref[:rows]
    image_ref[0] = base_ref[...] - 0.25 * (swap_ref[...] + off)


def body(fields, freq_index, slowness_index, slowness_table):
    rows, cols = slowness_index.shape[1:]
    slabs = lax.axis_size("slab")
    on_pairs = [(i, i + 1) for i in range(0, slabs - 1, 2)]
    off_pairs = [(i, i + 1) for i in range(1, slabs - 1, 2)]
    on_back = [(j, i) for i, j in on_pairs]
    off_back = [(j, i) for i, j in off_pairs]

    f32 = jnp.float32
    vmem = pl.BlockSpec(memory_space=pltpu.VMEM)
    hbm = pl.BlockSpec(memory_space=pltpu.HBM)
    products = 24 * (2 * rows) * cols * cols
    cost = pl.CostEstimate(flops=2 * products, bytes_accessed=16 * rows * cols * 4, transcendentals=0)

    long = pl.CostEstimate(
        flops=13 * products, bytes_accessed=104 * rows * cols * 4, transcendentals=0
    )

    def shape_of(height):
        return jax.ShapeDtypeStruct((height, cols), f32)

    def call(kernel, name, operands, out_shapes, cost=cost, **rest):
        rest.setdefault("in_specs", [vmem] * len(operands))
        rest.setdefault("out_specs", (vmem,) * len(out_shapes))
        return pl.pallas_call(
            kernel,
            out_shape=tuple(out_shapes),
            compiler_params=pltpu.CompilerParams(vmem_limit_bytes=32 * 1024 * 1024),
            cost_estimate=cost,
            name=name,
            **rest,
        )(*operands)

    long_state_shape = shape_of(4 * rows + 2 * EXTRA)
    state_shape, plane_shape, image_shape = shape_of(4 * rows + EXTRA), shape_of(rows + EXTRA), shape_of(rows)
    tables = [jnp.asarray(table) for table in dft_tables(rows, cols)]
    table_shapes = [jax.ShapeDtypeStruct(t.shape, t.dtype) for t in tables]
    levels_shape = jax.ShapeDtypeStruct((EXTRA,) + slowness_table.shape, f32)
    kept_shapes = [plane_shape, image_shape, shape_of(rows // 2 + EXTRA), levels_shape] + table_shapes
    loaded = (fields, slowness_index, slowness_table[None], *tables)
    operands = (freq_index,) + tuple(
        pltpu.with_memory_space_constraint(x, pltpu.HBM) for x in loaded
    )
    scratch = [
        pltpu.SMEM(freq_index.shape, freq_index.dtype),
        pltpu.VMEM(fields.shape, f32),
        pltpu.VMEM(slowness_index.shape, slowness_index.dtype),
        pltpu.VMEM((1,) + slowness_table.shape, f32),
        pltpu.SemaphoreType.DMA((4 + TABLES,)),
    ]
    odd_state, odd_plane, odd_image, *odd_constants = call(
        odd_first_kernel, "odd_first_step", operands, [long_state_shape] + kept_shapes,
        in_specs=[hbm] * len(operands), scratch_shapes=scratch,
    )
    from_off = lax.ppermute(odd_state, "slab", off_pairs)
    even_state, even_plane, even_image, *even_constants = call(
        even_first_kernel, "even_first_step", (*operands, odd_image), [state_shape] + kept_shapes,
        in_specs=[hbm] * len(operands) + [vmem], scratch_shapes=scratch,
    )
    from_on = lax.ppermute(even_state, "slab", on_pairs)
    next_plane = lax.ppermute(even_plane, "slab", off_back)
    odd_state, odd_image = call(
        odd_second_kernel, "odd_second_step", (from_on, odd_plane, odd_image, *odd_constants),
        [shape_of(4 * rows + 3 * EXTRA), image_shape], cost=None,
    )
    last_off = lax.ppermute(odd_state, "slab", off_pairs)
    even_state, even_image, up_image = call(
        even_arrival_kernel, "even_arrival_step", (from_off, even_plane, even_image, *even_constants),
        [state_shape, image_shape, shape_of(rows + 2 * EXTRA)],
    )
    last_on = lax.ppermute(even_state, "slab", on_pairs)
    below = lax.ppermute(up_image, "slab", off_back)
    (ahead,) = call(
        odd_ahead_kernel, "odd_step_ahead", (odd_state, next_plane, *odd_constants), [image_shape],
        cost=long,
    )
    odd_fields, odd_raw, odd_base = call(
        odd_last_kernel, "odd_last_step", (last_on, odd_plane, odd_image, ahead, *odd_constants),
        [shape_of(4 * rows), shape_of(rows + EXTRA), image_shape], cost=None,
    )
    above = lax.ppermute(odd_raw, "slab", off_pairs)
    even_fields, raw, base = call(
        even_last_kernel, "even_last_step",
        (last_off, even_plane, even_image, odd_raw, odd_base, *even_constants),
        [shape_of(4 * rows), image_shape, image_shape], cost=None,
    )
    swapped = lax.ppermute(raw, "slab", on_pairs + on_back)
    fields_out, done = call(
        write_kernel, "write_fields", (odd_fields, even_fields),
        [jax.ShapeDtypeStruct(fields.shape, f32), jax.ShapeDtypeStruct((EXTRA, LANES), f32)],
        out_specs=(hbm, vmem), scratch_shapes=[pltpu.SemaphoreType.DMA((4,))], cost=None,
    )
    (image,) = call(
        stencil_kernel, "image_stencil", (base, below, above, swapped, done),
        [jax.ShapeDtypeStruct((1, rows, cols), f32)], cost=None,
    )
    return image, fields_out


def solution(mesh):
    return jax.shard_map(
        body,
        mesh=mesh,
        in_specs=(
            P(("shots", "slab"), None, None, None, None),
            P(("shots", "slab")),
            P("slab", None, None),
            P(),
        ),
        out_specs=(P(("shots", "slab"), None, None), P(("shots", "slab"), None, None, None, None)),
        check_vma=False,
    )
```

```python
import functools
import math

import jax
import jax.numpy as jnp
import ml_dtypes
import numpy as np
from jax import lax
from jax.experimental import pallas as pl
from jax.experimental.pallas import tpu as pltpu
from jax.sharding import PartitionSpec as P

TICKS = 3
NFREQ = 512
EXTRA = 8
LANES = 128
TABLES = 2
TWO_PI = 2.0 * math.pi


def split_table(angle):
    parts = np.concatenate([np.cos(angle), np.sin(angle)], axis=0)
    high = parts.astype(np.float32).astype(ml_dtypes.bfloat16)
    low = (parts - high.astype(np.float64)).astype(np.float32).astype(ml_dtypes.bfloat16)
    return np.concatenate([high, low], axis=0)


def x_order(rows):
    front = np.arange(rows // 2)
    return np.concatenate([front, [rows // 2], rows - front[1:]])


def dft_tables(rows, cols):
    x_no, y_no = np.arange(rows), np.arange(cols // 2)
    to_x = np.outer(x_order(rows), x_no) % rows * (TWO_PI / rows)
    even = np.outer(y_no, 2 * y_no) % cols * (TWO_PI / cols)
    to_odd = np.outer(y_no, 2 * y_no + 1) % cols * (TWO_PI / cols)
    groups = ((to_x, to_x.T), (even, to_odd, to_odd.T))
    return [np.concatenate([split_table(angle) for angle in group]) for group in groups]


def table_views(x_ref, y_ref):
    views = []
    for ref, count in ((x_ref, 2), (y_ref, 3)):
        size = 4 * ref.shape[1]
        views += [ref.at[pl.ds(i * size, size)] for i in range(count)]
    return views


def halves(value):
    high = value.astype(jnp.bfloat16)
    return high, (value - high.astype(jnp.float32)).astype(jnp.bfloat16)


def dot(left, right):
    return jnp.dot(left, right, preferred_element_type=jnp.float32)


def table_parts(table_ref, turn):
    size = table_ref.shape[1]
    parts = []
    for start in (0, 2 * size):
        cos = table_ref[start : start + size]
        sin = table_ref[start + size : start + 2 * size]
        if turn:
            parts.append(stack(side(cos, sin), side(-sin, cos)))
        else:
            parts.append(stack(side(cos, -sin), side(sin, cos)))
    return parts


def dot_right(value, table_ref):
    table_high, table_low = table_parts(table_ref, False)
    high, low = halves(value)
    return dot(side(high, low, high), stack(table_high, table_high, table_low))


def dot_left(table_ref, value):
    table_high, table_low = table_parts(table_ref, True)
    high, low = halves(value)
    return dot(table_high, high) + (dot(table_low, high) + dot(table_high, low))


def cos_sin(angle):
    turns = jnp.floor(angle * (1.0 / math.pi) + 0.5)
    pairs = turns * 0.5
    flip = 1.0 - 4.0 * (pairs - jnp.floor(pairs))
    rest = angle - turns * math.pi
    sq = rest * rest
    sin = -1.98089830e-4 + sq * 2.60501962e-6
    sin = 8.33304978e-3 + sq * sin
    sin = -1.66666579e-1 + sq * sin
    sin = 9.99999996e-1 + sq * sin
    cos = -1.38535979e-3 + sq * 2.31515763e-5
    cos = 4.16635698e-2 + sq * cos
    cos = -4.99999047e-1 + sq * cos
    cos = 9.99999953e-1 + sq * cos
    return cos * flip, sin * (rest * flip)


def wave_square(rows, cols):
    half = cols // 2
    shape = (rows // 2 + EXTRA, cols)
    row = lax.broadcasted_iota(jnp.int32, shape, 0)
    row = jnp.where(row > rows // 2, rows // 2 - row, row)
    col = lax.broadcasted_iota(jnp.int32, shape, 1)
    col = jnp.where(col < half, 2 * col, 2 * (col - half) + 1)
    col = jnp.where(col < half, col, col - cols)
    wave_x = row.astype(jnp.float32) * (TWO_PI / rows)
    wave_y = col.astype(jnp.float32) * (TWO_PI / cols)
    return wave_x * wave_x + wave_y * wave_y


def depth_factor(omega_mean, wave_sq, rows, cols):
    gap = omega_mean * omega_mean - wave_sq
    root = jnp.sqrt(jnp.abs(gap))
    cos, sin = cos_sin(root)
    scale = 1.0 / (rows * cols)
    wave = gap > 0.0
    cos = jnp.where(wave, cos, jnp.exp(-root)) * scale
    sin = jnp.where(wave, sin, 0.0) * scale
    return [stack(part, part[EXTRA : rows // 2]) for part in (cos, sin)]


def side(*parts):
    return jnp.concatenate(parts, axis=1)


def stack(*parts):
    return jnp.concatenate(parts, axis=0)


def depth_step(fields, factor, screen, tables):
    left, left_back, even, odd, odd_back = table_views(*tables)
    spectra = []
    for real, imag in fields:
        half = real.shape[1] // 2
        first = side(real[:, :half], imag[:, :half])
        second = side(real[:, half:], imag[:, half:])
        spectra.append((dot_right(first + second, even), dot_right(first - second, odd)))
    spectra = [
        stack(side(low[:, :half], high[:, :half]), side(low[:, half:], high[:, half:]))
        for low, high in spectra
    ]
    spectra = [dot_left(left, spectrum) for spectrum in spectra]
    cos, sin = factor()
    rows = cos.shape[0]
    moved = []
    for spectrum in spectra:
        real, imag = spectrum[:rows], spectrum[rows:]
        moved.append(stack(real * sin + imag * cos, real * cos - imag * sin))
    backs = [dot_left(left_back, spectrum) for spectrum in moved]
    parts = []
    for back in backs:
        sum_part = dot_right(side(back[:rows, :half], back[rows:, :half]), even)
        gap_part = dot_right(side(back[:rows, half:], back[rows:, half:]), odd_back)
        parts.append((sum_part, gap_part))
    cos, sin = screen()
    results = []
    for sum_part, gap_part in parts:
        first, second = sum_part + gap_part, sum_part - gap_part
        real = side(first[:, half:], second[:, half:])
        imag = side(first[:, :half], second[:, :half])
        results.append((real * cos - imag * sin, real * sin + imag * cos))
    return results


def both_fields(state_ref, rows, factor, screen, tables):
    def fields():
        if len(state_ref.shape) == 2:
            parts = [state_ref[i * rows : (i + 1) * rows] for i in range(4)]
        else:
            parts = [state_ref[0, i, j] for i in range(2) for j in range(2)]
        s_real, s_imag, r_real, r_imag = parts
        return (s_real, s_imag), (r_imag, r_real)

    (s_real, s_imag), (r_imag, r_real) = depth_step(fields(), factor, screen, tables)
    return (s_real, s_imag, r_real, r_imag), s_real * r_real + s_imag * r_imag


def look_up(index, *tables):
    found = []
    for table in tables:
        pieces = []
        for start in range(0, index.shape[1], LANES):
            piece = index[:, start : start + LANES]
            value = jnp.zeros(piece.shape, jnp.float32)
            for low in range(0, table.shape[1], LANES):
                entries = jnp.broadcast_to(table[:, low : low + LANES], piece.shape)
                inside = jnp.clip(piece - low, 0, LANES - 1)
                picked = jnp.take_along_axis(entries, inside, axis=1)
                value = jnp.where(piece >= low, picked, value)
            pieces.append(value)
        found.append(side(*pieces))
    return found


def screen_of(index, omega, entries, mean):
    return look_up(index, *cos_sin(omega * (entries - mean)))


def store_planes(ref, planes):
    rows = planes[0].shape[0]
    for i, plane in enumerate(planes):
        ref[i * rows : (i + 1) * rows] = plane


def is_odd():
    return lax.rem(lax.axis_index("slab"), 2) == 1


def is_even():
    return jnp.logical_not(is_odd())


def load_and_step(operands, outputs, scratch):
    freq_hbm, fields_hbm, index_hbm, entries_hbm, *tables_hbm = operands
    state_ref, plane_ref, image_ref, wave_ref, levels_ref, *tables = outputs
    freq_ref, own_ref, index_ref, entries_ref, sems = scratch
    rows, cols = image_ref.shape
    pairs = [(fields_hbm, own_ref), (index_hbm, index_ref), (entries_hbm, entries_ref)]
    pairs += [(freq_hbm, freq_ref), *zip(tables_hbm, tables)]
    copies = [pltpu.make_async_copy(*pair, sems.at[i]) for i, pair in enumerate(pairs)]
    for copy in copies:
        copy.start()
    wave_sq = wave_square(rows, cols)
    wave_ref[...] = wave_sq
    for copy in copies:
        copy.wait()
    index, entries = index_ref[0], entries_ref[...]
    omega = 1.0 + freq_ref[0].astype(jnp.float32) * (1.0 / NFREQ)
    means = []

    def factor():
        (slow,) = look_up(index, entries)
        means.append(jnp.sum(slow, axis=(0, 1), keepdims=True) * (1.0 / (rows * cols)))
        return depth_factor(omega * means[0], wave_sq, rows, cols)

    planes, image = both_fields(
        own_ref, rows, factor, lambda: screen_of(index, omega, entries, means[0]), tables
    )
    store_planes(state_ref, planes)
    state_ref[4 * rows :] = jnp.full((state_ref.shape[0] - 4 * rows, cols), omega, jnp.float32)
    image_ref[...] = image
    plane_ref[:rows] = index.astype(jnp.float32)
    plane_ref[rows:] = jnp.broadcast_to(means[0], (EXTRA, cols))
    levels_ref[...] = jnp.broadcast_to(entries, levels_ref.shape)


def odd_first_kernel(*refs):
    operands, refs = refs[: 4 + TABLES], refs[4 + TABLES :]
    outputs, scratch = refs[: 5 + TABLES], refs[5 + TABLES :]
    pl.when(is_odd())(functools.partial(load_and_step, operands, outputs, scratch))


def even_first_kernel(*refs):
    operands, refs = refs[: 4 + TABLES], refs[5 + TABLES :]
    outputs, scratch = refs[: 5 + TABLES], refs[5 + TABLES :]
    pl.when(is_even())(functools.partial(load_and_step, operands, outputs, scratch))


def step_from(state_ref, plane_ref, constants):
    wave_ref, levels_ref, *tables = constants
    rows = plane_ref.shape[0] - EXTRA
    omega = state_ref[4 * rows : 4 * rows + 1, :1]
    mean = plane_ref[rows : rows + 1, :1]
    index = plane_ref[:rows].astype(jnp.int32)
    return both_fields(
        state_ref,
        rows,
        lambda: depth_factor(omega * mean, wave_ref[...], rows, index.shape[1]),
        lambda: screen_of(index, omega, levels_ref[:1], mean),
        tables,
    )


def odd_second_kernel(state_in_ref, plane_ref, image_in_ref, *refs):
    constants, (state_ref, image_ref) = refs[: 2 + TABLES], refs[2 + TABLES :]
    rows = image_ref.shape[0]

    @pl.when(is_odd())
    def _():
        planes, image = step_from(state_in_ref, plane_ref, constants)
        store_planes(state_ref, planes)
        for start in range(4 * rows, state_ref.shape[0], EXTRA):
            state_ref[start : start + EXTRA] = state_in_ref[4 * rows :]
        image_ref[...] = image_in_ref[...] + image


def odd_ahead_kernel(state_in_ref, plane_ref, *refs):
    constants, (image_ref,) = refs[: 2 + TABLES], refs[2 + TABLES :]
    has_next = is_odd() & (lax.axis_index("slab") < lax.axis_size("slab") - 1)

    @pl.when(has_next)
    def _():
        _, image = step_from(state_in_ref, plane_ref, constants)
        image_ref[...] = image

    @pl.when(jnp.logical_not(has_next))
    def _():
        image_ref[...] = jnp.zeros_like(image_ref)


def fill_wide(ref, raw):
    rows = raw.shape[0]
    ref[:rows] = raw
    ref[rows:] = jnp.zeros((ref.shape[0] - rows, ref.shape[1]), jnp.float32)


def even_arrival_kernel(state_in_ref, plane_ref, image_in_ref, *refs):
    constants, (state_ref, image_ref, up_ref) = refs[: 2 + TABLES], refs[2 + TABLES :]
    rows = image_ref.shape[0]

    @pl.when(is_even())
    def _():
        planes, image = step_from(state_in_ref, plane_ref, constants)
        store_planes(state_ref, planes)
        state_ref[4 * rows :] = state_in_ref[4 * rows : 4 * rows + EXTRA]
        image = image_in_ref[...] + image
        image_ref[...] = image
        fill_wide(up_ref, image)


def odd_last_kernel(state_in_ref, plane_ref, image_in_ref, ahead_ref, *refs):
    constants, (state_ref, raw_ref, base_ref) = refs[: 2 + TABLES], refs[2 + TABLES :]

    @pl.when(is_odd())
    def _():
        planes, image = step_from(state_in_ref, plane_ref, constants)
        store_planes(state_ref, planes)
        raw = image_in_ref[...] + image
        fill_wide(raw_ref, raw)
        base_ref[...] = raw - 0.25 * ahead_ref[...]


def even_last_kernel(
    state_in_ref, plane_ref, image_in_ref, odd_raw_ref, odd_base_ref, *refs
):
    constants, (state_ref, raw_ref, base_ref) = refs[: 2 + TABLES], refs[2 + TABLES :]

    @pl.when(is_even())
    def _():
        planes, image = step_from(state_in_ref, plane_ref, constants)
        store_planes(state_ref, planes)
        raw = image_in_ref[...] + image
        raw_ref[...] = raw
        base_ref[...] = raw

    @pl.when(is_odd())
    def _():
        raw_ref[...] = odd_raw_ref[: raw_ref.shape[0]]
        base_ref[...] = odd_base_ref[...]


def write_kernel(odd_ref, even_ref, fields_hbm, done_ref, sems):
    rows = even_ref.shape[0] // 4

    def write(ref):
        copies = [
            pltpu.make_async_copy(
                ref.at[pl.ds(i * rows, rows)], fields_hbm.at[0, i // 2, i % 2], sems.at[i]
            )
            for i in range(4)
        ]
        for copy in copies:
            copy.start()
        for copy in copies:
            copy.wait()

    pl.when(is_odd())(functools.partial(write, odd_ref))
    pl.when(is_even())(functools.partial(write, even_ref))
    done_ref[...] = jnp.zeros_like(done_ref)


def stencil_kernel(base_ref, below_ref, above_ref, swap_ref, done_ref, image_ref):
    del done_ref
    rows = base_ref.shape[0]
    off = below_ref[:rows] + above_ref[:rows]
    image_ref[0] = base_ref[...] - 0.25 * (swap_ref[...] + off)


def body(fields, freq_index, slowness_index, slowness_table):
    rows, cols = slowness_index.shape[1:]
    slabs = lax.axis_size("slab")
    on_pairs = [(i, i + 1) for i in range(0, slabs - 1, 2)]
    off_pairs = [(i, i + 1) for i in range(1, slabs - 1, 2)]
    on_back = [(j, i) for i, j in on_pairs]
    off_back = [(j, i) for i, j in off_pairs]

    f32 = jnp.float32
    vmem = pl.BlockSpec(memory_space=pltpu.VMEM)
    hbm = pl.BlockSpec(memory_space=pltpu.HBM)
    products = 24 * (2 * rows) * cols * cols
    cost = pl.CostEstimate(flops=2 * products, bytes_accessed=16 * rows * cols * 4, transcendentals=0)

    long = pl.CostEstimate(
        flops=13 * products, bytes_accessed=104 * rows * cols * 4, transcendentals=0
    )

    def shape_of(height):
        return jax.ShapeDtypeStruct((height, cols), f32)

    def call(kernel, name, operands, out_shapes, cost=cost, **rest):
        rest.setdefault("in_specs", [vmem] * len(operands))
        rest.setdefault("out_specs", (vmem,) * len(out_shapes))
        return pl.pallas_call(
            kernel,
            out_shape=tuple(out_shapes),
            compiler_params=pltpu.CompilerParams(vmem_limit_bytes=32 * 1024 * 1024),
            cost_estimate=cost,
            name=name,
            **rest,
        )(*operands)

    long_state_shape = shape_of(4 * rows + 2 * EXTRA)
    state_shape, plane_shape, image_shape = shape_of(4 * rows + EXTRA), shape_of(rows + EXTRA), shape_of(rows)
    tables = [jnp.asarray(table) for table in dft_tables(rows, cols)]
    table_shapes = [jax.ShapeDtypeStruct(t.shape, t.dtype) for t in tables]
    levels_shape = jax.ShapeDtypeStruct((EXTRA,) + slowness_table.shape, f32)
    kept_shapes = [plane_shape, image_shape, shape_of(rows // 2 + EXTRA), levels_shape] + table_shapes
    loaded = (fields, slowness_index, slowness_table[None], *tables)
    operands = (freq_index,) + tuple(
        pltpu.with_memory_space_constraint(x, pltpu.HBM) for x in loaded
    )
    scratch = [
        pltpu.SMEM(freq_index.shape, freq_index.dtype),
        pltpu.VMEM(fields.shape, f32),
        pltpu.VMEM(slowness_index.shape, slowness_index.dtype),
        pltpu.VMEM((1,) + slowness_table.shape, f32),
        pltpu.SemaphoreType.DMA((4 + TABLES,)),
    ]
    odd_state, odd_plane, odd_image, *odd_constants = call(
        odd_first_kernel, "odd_first_step", operands, [long_state_shape] + kept_shapes,
        in_specs=[hbm] * len(operands), scratch_shapes=scratch,
    )
    from_off = lax.ppermute(odd_state, "slab", off_pairs)
    even_state, even_plane, even_image, *even_constants = call(
        even_first_kernel, "even_first_step", (*operands, odd_image), [state_shape] + kept_shapes,
        in_specs=[hbm] * len(operands) + [vmem], scratch_shapes=scratch,
    )
    from_on = lax.ppermute(even_state, "slab", on_pairs)
    next_plane = lax.ppermute(even_plane, "slab", off_back)
    odd_state, odd_image = call(
        odd_second_kernel, "odd_second_step", (from_on, odd_plane, odd_image, *odd_constants),
        [shape_of(4 * rows + 3 * EXTRA), image_shape], cost=None,
    )
    last_off = lax.ppermute(odd_state, "slab", off_pairs)
    even_state, even_image, up_image = call(
        even_arrival_kernel, "even_arrival_step", (from_off, even_plane, even_image, *even_constants),
        [state_shape, image_shape, shape_of(rows + 2 * EXTRA)],
    )
    last_on = lax.ppermute(even_state, "slab", on_pairs)
    below = lax.ppermute(up_image, "slab", off_back)
    (ahead,) = call(
        odd_ahead_kernel, "odd_step_ahead", (odd_state, next_plane, *odd_constants), [image_shape],
        cost=long,
    )
    odd_fields, odd_raw, odd_base = call(
        odd_last_kernel, "odd_last_step", (last_on, odd_plane, odd_image, ahead, *odd_constants),
        [shape_of(4 * rows), shape_of(rows + EXTRA), image_shape], cost=None,
    )
    above = lax.ppermute(odd_raw, "slab", off_pairs)
    even_fields, raw, base = call(
        even_last_kernel, "even_last_step",
        (last_off, even_plane, even_image, odd_raw, odd_base, *even_constants),
        [shape_of(4 * rows), image_shape, image_shape], cost=None,
    )
    swapped = lax.ppermute(raw, "slab", on_pairs + on_back)
    fields_out, done = call(
        write_kernel, "write_fields", (odd_fields, even_fields),
        [jax.ShapeDtypeStruct(fields.shape, f32), jax.ShapeDtypeStruct((EXTRA, LANES), f32)],
        out_specs=(hbm, vmem), scratch_shapes=[pltpu.SemaphoreType.DMA((4,))], cost=None,
    )
    (image,) = call(
        stencil_kernel, "image_stencil", (base, below, above, swapped, done),
        [jax.ShapeDtypeStruct((1, rows, cols), f32)], cost=None,
    )
    return image, fields_out


def solution(mesh):
    return jax.shard_map(
        body,
        mesh=mesh,
        in_specs=(
            P(("shots", "slab"), None, None, None, None),
            P(("shots", "slab")),
            P("slab", None, None),
            P(),
        ),
        out_specs=(P(("shots", "slab"), None, None), P(("shots", "slab"), None, None, None, None)),
        check_vma=False,
    )
```
